256 devices in a mesh: kv: 8 (over y, x_hi), ctx: 32 (over z, x_lo, core).
Axes of the slice: x: 4 (x_hi: 2, x_lo: 2; x = x_hi * 2 + x_lo), y: 4, z: 8, core: 2. Of those that a mesh axis runs over, the one named last changes fastest.
Arguments:
- queries: bfloat16 [8192, 64, 128], P(('ctx', 'kv')), may hold values from -9 to 9
- keys: bfloat16 [8192, 8, 128], P(('ctx', 'kv')), may hold values from -5 to 5
- values: bfloat16 [8192, 8, 128], P(('ctx', 'kv')), may hold values from -6 to 6
- offsets: int32 [8192, 8, 128], P(('ctx', 'kv')), may hold values from 0 to 255
- smooth_exp: int32 [8, 128], replicated, may hold values from -1 to 1
- scale_exp: int32 [8, 128], replicated, may hold values from -6 to -5
- placement: int32 [8192], replicated, may hold values from 0 to 8191, as said below
- doc_lengths: int32 [16], replicated, may hold values from 1 to 2048, 8192 in all
Outputs:
- attended: bfloat16 [8192, 64, 128], P(('ctx', 'kv'))
The draws below stay inside these ranges and needn't reach their ends.
Inputs may be any that keep to these rules, and one draw needn't show every extreme that they name: `placement`: each aligned run of 32 entries holds 32 consecutive positions starting at a multiple of 32; every position appears once.
All inputs are finite; a program needn't handle non-finite values.
Results may differ from the reference program's by a relative error of at most 0.008.
Values may be sent and summed in bfloat16 or wider, within the bound.
A program may use at most 64 MiB of HBM per device.

```python
import math
import jax
import jax.numpy as jnp
import numpy as np
from jax import lax

Q_HEADS = 64
KV_HEADS = 8
HEAD_DIM = 128
BLOCK = 32
DOCS = 16
SEQ = 8192


def draw_queries(key, part):
    key = jax.random.fold_in(key, 2)
    drawn = jnp.clip(jax.random.normal(key, (SEQ, Q_HEADS, HEAD_DIM), jnp.float32), -6.0, 6.0)
    return drawn.astype(jnp.bfloat16)


def draw_keys(key, part):
    key = jax.random.fold_in(key, 3)
    drawn = jnp.clip(jax.random.normal(key, (SEQ, KV_HEADS, HEAD_DIM), jnp.float32), -5.0, 5.0)
    return drawn.astype(jnp.bfloat16)


def draw_placement(key, part):
    key = jax.random.fold_in(key, 1)
    order = jax.random.permutation(key, SEQ // BLOCK).astype(jnp.int32)
    inside = jnp.arange(BLOCK, dtype=jnp.int32)
    return (order[:, None] * BLOCK + inside[None, :]).reshape(SEQ).astype(jnp.int32)


def place_ends(array, own_key, low, high):
    dims = array.shape
    spot = [jax.random.randint(jax.random.fold_in(own_key, axis), (), 0, dims[axis]) for axis in range(len(dims))]
    array = array.at[tuple(spot)].set(low)
    longest = dims.index(max(dims))
    spot[longest] = (spot[longest] + 1) % dims[longest]
    return array.at[tuple(spot)].set(high)


def shard_levels(key, dims, split, low, largest):
    loudness, own = 1.0, jax.random.fold_in(key, 6)
    for position, blocks in split:
        heights = jnp.exp(jax.random.uniform(jax.random.fold_in(own, position), (blocks,), jnp.float32, low / len(split), largest / len(split)))
        loudness = loudness * jnp.repeat(heights, dims[position] // blocks).reshape([-1 if axis == position else 1 for axis in range(len(dims))])
    return loudness


def profile(count, total, reach, lean):
    loads = [(1 << 20) // math.isqrt(rank ** lean) + 1 for rank in range(2, count + 1)]
    surplus, holding = total - reach - (count - 1), [1] * (count - 1)
    while surplus > 0:
        candidates = [i for i in range(count - 1) if holding[i] < reach]
        pool, left = sum([loads[i] for i in candidates]), surplus
        for i in candidates:
            extra = min(reach - holding[i], max(1, left * loads[i] // pool), surplus)
            holding[i] = holding[i] + extra
            surplus = surplus - extra
    return np.array([reach] + holding)


def ragged_sizes(stream_key, amount, total, bound, skew):
    if amount == 2:
        one = jax.random.randint(stream_key, (), max(1, total - bound), min(bound, total - 1) + 1)
        return jnp.stack([one, total - one])
    sizes = jnp.asarray(profile(amount, total, bound, skew), jnp.int32)
    pairs = (amount - 1) // 2
    giver, taker = sizes[1:1 + 2 * pairs:2], sizes[2:2 + 2 * pairs:2]
    slack = jnp.minimum(giver - 1, bound - taker)
    shifted = jax.random.randint(jax.random.fold_in(stream_key, 1), (pairs,), 0, 1 << 20) % (slack + 1)
    sizes = sizes.at[1:1 + 2 * pairs:2].set(giver - shifted).at[2:2 + 2 * pairs:2].set(taker + shifted)
    return sizes[jax.random.permutation(jax.random.fold_in(stream_key, 2), amount)]


def bell_draw(rng, dims, deviation, most, split=(), kind=jnp.bfloat16):
    gain = shard_levels(rng, dims, split, -0.22, 0.18) if split else 1.0
    entries = jax.random.normal(rng, dims, jnp.float32) * deviation * gain
    return jnp.minimum(jnp.maximum(entries, -most), most).astype(kind)


def setup_inputs(seed: int = 0) -> dict:
    key_of = jax.random.split(jax.random.key(seed), 9)
    queries = draw_queries(jax.random.fold_in(key_of[8], 71), 0)
    keys = draw_keys(jax.random.fold_in(key_of[8], 71), 0)
    values = bell_draw(key_of[2], (SEQ, KV_HEADS, HEAD_DIM), 1.0, 6.0, ((0, 256),))
    offsets = place_ends(jax.random.randint(key_of[3], (SEQ, KV_HEADS, HEAD_DIM), 0, 256), jax.random.fold_in(key_of[3], 1), 0, 255).astype(jnp.int32)
    smooth_exp = place_ends(jax.random.randint(key_of[4], (KV_HEADS, HEAD_DIM), -1, 2), jax.random.fold_in(key_of[4], 1), -1, 1).astype(jnp.int32)
    scale_exp = place_ends(jax.random.randint(key_of[5], (KV_HEADS, HEAD_DIM), -6, -4), jax.random.fold_in(key_of[5], 1), -6, (-4) - 1).astype(jnp.int32)
    placement = draw_placement(jax.random.fold_in(key_of[8], 71), 0)
    doc_lengths = ragged_sizes(key_of[7], DOCS, SEQ, SEQ // 4, 2).astype(jnp.int32)
    return dict(queries=queries, keys=keys, values=values, offsets=offsets, smooth_exp=smooth_exp, scale_exp=scale_exp, placement=placement, doc_lengths=doc_lengths)


def quant_keys(keys, smooth_exp, scale_exp, offsets):
    shift_all = jnp.left_shift(jnp.int32(1), (-(smooth_exp + scale_exp)).astype(jnp.int32)).astype(jnp.float32)
    key_codes = jnp.floor(keys.astype(jnp.float32) * shift_all + offsets.astype(jnp.float32) / 256.0)
    key_codes = jnp.clip(key_codes, -128.0, 127.0)
    shift_back = jnp.left_shift(jnp.int32(1), (-scale_exp).astype(jnp.int32)).astype(jnp.float32)
    return (key_codes / shift_back).astype(jnp.bfloat16)


def scale_queries(queries, smooth_exp):
    lifted = jnp.left_shift(jnp.int32(1), (smooth_exp + 1).astype(jnp.int32)).astype(jnp.float32) * 0.5
    group = queries.shape[1] // smooth_exp.shape[0]
    lifted = jnp.repeat(lifted, group, axis=0)
    return (queries.astype(jnp.float32) * lifted).astype(jnp.bfloat16)


def doc_of(positions, doc_lengths):
    doc_ends = jnp.cumsum(doc_lengths).astype(jnp.int32)
    return jnp.sum((positions[:, None] >= doc_ends[None, :]).astype(jnp.int32), axis=1).astype(jnp.int32)


def reference(queries, keys, values, offsets, smooth_exp, scale_exp, placement, doc_lengths):
    scaled = scale_queries(queries, smooth_exp)
    coded = quant_keys(keys, smooth_exp, scale_exp, offsets)
    doc_ids = doc_of(placement, doc_lengths)
    group = Q_HEADS // KV_HEADS
    grouped = scaled.reshape(SEQ, KV_HEADS, group, HEAD_DIM)
    query_rows = min(512, SEQ)
    factor = HEAD_DIM ** -0.5

    def per_head(head):
        head_queries = grouped[:, head]
        head_keys = coded[:, head].astype(jnp.float32)
        head_values = values[:, head].astype(jnp.float32)

        def per_block(block):
            first_row = (block * query_rows).astype(jnp.int32)
            block_queries = lax.dynamic_slice_in_dim(head_queries, first_row, query_rows, 0).astype(jnp.float32)
            pos_query = lax.dynamic_slice_in_dim(placement, first_row, query_rows, 0)
            doc_query = lax.dynamic_slice_in_dim(doc_ids, first_row, query_rows, 0)
            scores = jnp.einsum("qgd,kd->gqk", block_queries, head_keys) * factor
            allowed = (placement[None, :] <= pos_query[:, None]) & (doc_ids[None, :] == doc_query[:, None])
            scores = jnp.where(allowed[None], scores, -1e30)
            row_max = jnp.max(scores, axis=-1)
            weights = jnp.where(allowed[None], jnp.exp(scores - row_max[..., None]), 0.0).astype(jnp.bfloat16)
            wide_weights = weights.astype(jnp.float32)
            denom = jnp.sum(wide_weights, axis=-1)
            result = jnp.einsum("gqk,kd->gqd", wide_weights, head_values) / denom[..., None]
            return jnp.transpose(result.astype(jnp.bfloat16), (1, 0, 2))

        blocks = lax.map(per_block, jnp.arange(SEQ // query_rows, dtype=jnp.int32))
        return blocks.reshape(SEQ, group, HEAD_DIM)

    heads = lax.map(per_head, jnp.arange(KV_HEADS, dtype=jnp.int32))
    return jnp.transpose(heads, (1, 0, 2, 3)).reshape(SEQ, Q_HEADS, HEAD_DIM)
```

```python
import jax
import jax.numpy as jnp
from jax import lax
from jax.experimental import pallas as pl
from jax.experimental.pallas import tpu as pltpu
from jax.sharding import PartitionSpec as P

MESH = pl.DeviceIdType.MESH
TOK = 32
HEADS = 8
GROUP = 8
DIM = 128
BLOCKS = 256
REACH = 64
WIN = (REACH + 1) * TOK
PAD = 2176
CHUNK = 256
FACTOR = DIM**-0.5 * 1.4426950408889634
LOW = -1e30


def spot(x, y, z, core):
    return (y * 2 + x // 2, z * 4 + (x % 2) * 2 + core)


def kernel(
    order, block_pos, doc_lengths, q_ref, k_ref, v_ref, off_ref, smooth_ref, scale_ref, out_ref,
    rows, kv_send, kv_all, q_send, q_all, o_send, o_all, thr, kwin, vwin, scores,
    kvs, kvr, qs, qr, os, orr, gs, gr,
):
    kv = lax.axis_index("kv")
    ctx = lax.axis_index("ctx")
    y, z, core = kv // 2, ctx // 4, ctx % 2
    x = (kv % 2) * 2 + (ctx // 2) % 2

    def along_z(o):
        return spot(x, y, lax.rem(z + o, 8), core)

    x_next = [spot((x + d) % 4, y, z, core) for d in (1, 3)]
    y_next = [spot(x, (y + d) % 4, z, core) for d in (1, 3)]
    twin = spot(x, y, z, 1 - core)
    greeted = [along_z(o) for o in range(1, 8)] + x_next + y_next + [twin]
    barrier = pltpu.get_barrier_semaphore()
    for peer in greeted:
        pl.semaphore_signal(barrier, inc=1, device_id=peer, device_id_type=MESH)

    exps = smooth_ref[...] + scale_ref[...]
    up = jnp.left_shift(jnp.int32(1), -exps).astype(jnp.float32)
    down = jnp.left_shift(jnp.int32(1), exps + 7).astype(jnp.float32) * (2.0**-7)
    codes = jnp.floor(
        k_ref[...].astype(jnp.float32) * up[None] + off_ref[...].astype(jnp.float32) * (1.0 / 256)
    )
    coded = jnp.clip(codes, -128.0, 127.0) * down[None]
    rows[0] = coded.reshape(TOK * HEADS, DIM)
    rows[1] = v_ref[...].astype(jnp.float32).reshape(TOK * HEADS, DIM)
    for h in range(HEADS):
        for t in range(2):
            kv_send[h, t] = rows[t, pl.ds(h, TOK, stride=HEADS), :].astype(jnp.bfloat16)

    pl.semaphore_wait(barrier, len(greeted))

    far_first = (4, 3, 5, 2, 6, 1, 7)
    kv_copies = []
    for o in far_first:
        c = pltpu.make_async_remote_copy(
            kv_send.at[lax.rem(z + o, 8)], kv_all.at[core, y, x, 8 - o],
            kvs.at[o], kvr.at[8 - o], device_id=along_z(o), device_id_type=MESH,
        )
        c.start()
        kv_copies.append(c)
    kv_all[core, y, x, 0] = kv_send[z]

    for g in range(HEADS // 2):
        pair = q_ref[:, 16 * g : 16 * g + 16, :].astype(jnp.float32)
        for i in range(2):
            q_send[2 * g + i] = (
                pair[:, 8 * i : 8 * i + 8, :].reshape(TOK * GROUP, DIM).astype(jnp.bfloat16)
            )
    q_copies = []
    for o in far_first:
        c = pltpu.make_async_remote_copy(
            q_send.at[lax.rem(z + o, 8)], q_all.at[8 - o],
            qs.at[o], qr.at[8 - o], device_id=along_z(o), device_id_type=MESH,
        )
        c.start()
        q_copies.append(c)
    q_all[0] = q_send[z]

    def block_at(o):
        return block_pos[lax.rem(z + o, 8) * 32 + (x % 2) * 16 + core * 8 + y * 2 + x // 2]

    def starts(o, carry):
        base = block_at(o) * TOK
        pos = base + lax.broadcasted_iota(jnp.int32, (TOK * GROUP, DIM), 0) // GROUP
        first = jnp.zeros((TOK * GROUP, DIM), jnp.int32)
        end = jnp.int32(0)
        for d in range(15):
            end = end + doc_lengths[d]
            first = jnp.where(pos >= end, end, first)
        thr[o] = first - (base - REACH * TOK)
        return carry

    lax.fori_loop(0, 8, starts, 0)
    vwin[:, DIM:] = jnp.ones((PAD, DIM), jnp.bfloat16)
    vwin[WIN:, :DIM] = jnp.zeros((PAD - WIN, DIM), jnp.bfloat16)
    kwin[WIN:] = jnp.zeros((PAD - WIN, DIM), jnp.bfloat16)

    for c in kv_copies:
        c.wait_recv()

    sends = []

    def send(ref, target):
        i = len(sends)
        c = pltpu.make_async_remote_copy(
            ref, ref, gs.at[i], gr.at[i], device_id=target, device_id_type=MESH
        )
        c.start()
        sends.append(c)
        return c

    nexts = {"x": x_next, "y": y_next}
    parts = (("x", "y", 0), ("y", "x", 4))

    def piece(rel, lo, n):
        return kv_all.at[core, (y + rel[1] + 4) % 4, (x + rel[0] + 4) % 4, pl.ds(lo, n)]

    def both(axis, rel, lo):
        return [send(piece(rel, lo, 4), target) for target in nexts[axis]]

    def moved(rel, axis, d):
        return (rel[0] + d, rel[1]) if axis == "x" else (rel[0], rel[1] + d)

    def pass_on(axis, rel, lo, copies):
        copies[0].wait_recv()
        a = send(piece(moved(rel, axis, -1), lo, 2), nexts[axis][0])
        copies[1].wait_recv()
        b = send(piece(moved(rel, axis, 1), lo + 2, 2), nexts[axis][1])
        return [a, b]

    twin_copies = []

    def line_to_twin(second, rel, lo):
        if second == "y":
            ref = kv_all.at[core, :, (x + rel[0] + 4) % 4, pl.ds(lo, 4)]
        else:
            ref = kv_all.at[core, (y + rel[1] + 4) % 4, :, pl.ds(lo, 4)]
        twin_copies.append(send(ref, twin))

    one = [both(p[0], (0, 0), p[2]) for p in parts]
    two = [(p, (0, 0), both(p[1], (0, 0), p[2])) for p in parts]
    opposite = [pass_on(p[0], (0, 0), p[2], c) for p, c in zip(parts, one)]
    for d in (-1, 1):
        for p in parts:
            rel = moved((0, 0), p[0], d)
            two.append((p, rel, both(p[1], rel, p[2])))
    last = []

    def second(entry):
        p, rel, copies = entry
        last.append((p, rel, pass_on(p[1], rel, p[2], copies)))

    def finish(entry):
        p, rel, copies = entry
        for c in copies:
            c.wait_recv()
        line_to_twin(p[1], rel, p[2])

    second(two[0])
    second(two[1])
    for p, copies in zip(parts, opposite):
        for c in copies:
            c.wait_recv()
        rel = moved((0, 0), p[0], 2)
        two.append((p, rel, both(p[1], rel, p[2])))
    for i in range(2, len(two)):
        second(two[i])
        finish(last[i - 2])
    for entry in last[len(two) - 2 :]:
        finish(entry)
    for c in twin_copies:
        c.wait_recv()
    for c in q_copies:
        c.wait_recv()

    lane = lax.broadcasted_iota(jnp.int32, (TOK * GROUP, DIM), 1)
    row = lax.broadcasted_iota(jnp.int32, (TOK * GROUP, DIM), 0)
    causal = lane <= row // GROUP

    def attend(j, carry):
        half, odd = j // 2, j % 2
        o = 4 + half - odd * (1 + 2 * half)
        pos = block_at(o)

        def fetch(i, c):
            for u in range(5):
                b = order[pos + i * 5 + u]
                src = kv_all.at[b // 128, (b // 32) % 4, (b // 8) % 4, b % 8]
                at = pl.ds(pl.multiple_of((i * 5 + u) * TOK, TOK), TOK)
                kwin[at, :] = src[0]
                vwin[at, pl.ds(0, DIM)] = src[1]
            return c

        lax.fori_loop(0, (REACH + 1) // 5, fetch, 0)
        q = q_all[o]
        first = thr[o]
        top = jnp.full((TOK * GROUP, DIM), LOW, jnp.float32)
        for c0 in range(0, PAD, CHUNK):
            width = min(CHUNK, PAD - c0)
            s = lax.dot_general(
                q, kwin[c0 : c0 + width, :], (((1,), (1,)), ((), ())),
                preferred_element_type=jnp.float32,
            )
            for t in range(0, width, DIM):
                ok = lane + (c0 + t) >= first
                if c0 + t == REACH * TOK:
                    ok = ok & causal
                tile = jnp.where(ok, s[:, t : t + DIM], LOW)
                scores[:, c0 + t : c0 + t + DIM] = tile
                top = jnp.maximum(top, tile)
        peak = jnp.max(top, axis=1, keepdims=True)
        total = jnp.zeros((TOK * GROUP, 2 * DIM), jnp.float32)
        for c0 in range(0, PAD, CHUNK):
            width = min(CHUNK, PAD - c0)
            w = jnp.exp2((scores[:, c0 : c0 + width] - peak) * FACTOR).astype(jnp.bfloat16)
            total = total + jnp.dot(
                w, vwin[c0 : c0 + width, :], preferred_element_type=jnp.float32
            )
        result = (total[:, :DIM] / total[:, DIM:]).astype(jnp.bfloat16)
        o_send[o] = result

        @pl.when(j < 7)
        def _():
            pltpu.make_async_remote_copy(
                o_send.at[o], o_all.at[z], os.at[o], orr.at[lax.rem(8 - o, 8)],
                device_id=along_z(o), device_id_type=MESH,
            ).start()

        return carry

    lax.fori_loop(0, 8, attend, 0)
    o_all[z] = o_send[0]
    for o in far_first:
        pltpu.make_async_remote_copy(
            o_send.at[o], o_all.at[z], os.at[o], orr.at[8 - o],
            device_id=along_z(o), device_id_type=MESH,
        ).wait_recv()
    for g in range(HEADS // 2):
        pair = [
            o_all[2 * g + i].astype(jnp.float32).reshape(TOK, GROUP, DIM) for i in range(2)
        ]
        out_ref[:, 16 * g : 16 * g + 16, :] = jnp.concatenate(pair, axis=1).astype(jnp.bfloat16)
    for c in kv_copies + q_copies + sends:
        c.wait_send()
    for o in far_first:
        pltpu.make_async_remote_copy(
            o_send.at[o], o_all.at[z], os.at[o], orr.at[8 - o],
            device_id=along_z(o), device_id_type=MESH,
        ).wait_send()


def shards(queries, keys, values, offsets, smooth_exp, scale_exp, placement, doc_lengths):
    z = lax.axis_index("ctx") // 4
    block_pos = placement.reshape(BLOCKS, TOK)[:, 0] // TOK
    b = jnp.arange(BLOCKS, dtype=jnp.int32)
    ctx, kv = b // 8, b % 8
    x = (kv % 2) * 2 + (ctx // 2) % 2
    place = (((ctx % 2) * 4 + kv // 2) * 4 + x) * 8 + (ctx // 4 - z) % 8
    order = jnp.sum(
        jnp.where(block_pos[None, :] == b[:, None], place[None, :], 0), axis=1
    ).astype(jnp.int32)
    order = jnp.concatenate([jnp.zeros((REACH,), jnp.int32), order])
    bf, f32 = jnp.bfloat16, jnp.float32
    dma = pltpu.SemaphoreType.DMA
    smem = pl.BlockSpec(memory_space=pltpu.SMEM)
    vmem = pl.BlockSpec(memory_space=pltpu.VMEM)
    n_rows = TOK * GROUP
    return pl.pallas_call(
        kernel,
        out_shape=jax.ShapeDtypeStruct(queries.shape, bf),
        in_specs=[smem] * 3 + [vmem] * 6,
        out_specs=vmem,
        scratch_shapes=[
            pltpu.VMEM((2, TOK * HEADS, DIM), f32),
            pltpu.VMEM((HEADS, 2, TOK, DIM), bf),
            pltpu.VMEM((2, 4, 4, 8, 2, TOK, DIM), bf),
            pltpu.VMEM((HEADS, n_rows, DIM), bf),
            pltpu.VMEM((8, n_rows, DIM), bf),
            pltpu.VMEM((8, n_rows, DIM), bf),
            pltpu.VMEM((HEADS, n_rows, DIM), bf),
            pltpu.VMEM((8, n_rows, DIM), jnp.int32),
            pltpu.VMEM((PAD, DIM), bf),
            pltpu.VMEM((PAD, 2 * DIM), bf),
            pltpu.VMEM((n_rows, PAD), f32),
            dma((8,)), dma((8,)), dma((8,)), dma((8,)), dma((8,)), dma((8,)),
            dma((48,)), dma((48,)),
        ],
        compiler_params=pltpu.CompilerParams(
            collective_id=0, has_side_effects=True, vmem_limit_bytes=40 * 2**20
        ),
        name="attend",
    )(order, block_pos, doc_lengths, queries, keys, values, offsets, smooth_exp, scale_exp)


def solution(mesh):
    tokens = P(("ctx", "kv"), None, None)
    return jax.shard_map(
        shards,
        mesh=mesh,
        in_specs=(tokens,) * 4 + (P(),) * 4,
        out_specs=tokens,
        check_vma=False,
    )
```

```python
import jax
import jax.numpy as jnp
from jax import lax
from jax.experimental import pallas as pl
from jax.experimental.pallas import tpu as pltpu
from jax.sharding import PartitionSpec as P

MESH = pl.DeviceIdType.MESH
TOK = 32
HEADS = 8
GROUP = 8
DIM = 128
BLOCKS = 256
REACH = 64
PAD = 2176
CHUNK = 256
N_ROWS = TOK * GROUP
SORTED = REACH + BLOCKS + 8
DOCS = 16
BIG = 65536.0
FACTOR = DIM**-0.5 * 1.4426950408889634
LOW = -1e30


def spot(x, y, z, core):
    return (y * 2 + x // 2, z * 4 + (x % 2) * 2 + core)


def kernel(
    place_hbm, docs_hbm, q_hbm, k_hbm, v_hbm, off_hbm, smooth_hbm, scale_hbm, out_ref,
    place_v, place_s, docs_s, q_ref, k_ref, v_ref, off_ref, smooth_ref, scale_ref, order_v, order,
    rows, kv_send, kv_all, q_send, q_all, q_doc, o_send, o_all, keys, vals, scores,
    kvs, kvr, qs, qr, os, orr, gs, gr, ins,
):
    loads = []
    pairs = (
        (k_hbm, k_ref), (off_hbm, off_ref), (smooth_hbm, smooth_ref), (scale_hbm, scale_ref),
        (v_hbm, v_ref), (q_hbm, q_ref), (docs_hbm, docs_s), (place_hbm, place_v),
        (place_hbm, place_s),
    )
    for i, (src, dst) in enumerate(pairs):
        c = pltpu.make_async_copy(src, dst, ins.at[i])
        c.start()
        loads.append(c)
    kv = lax.axis_index("kv")
    ctx = lax.axis_index("ctx")
    y, z, core = kv // 2, ctx // 4, ctx % 2
    x = (kv % 2) * 2 + (ctx // 2) % 2

    def along_z(o):
        return spot(x, y, lax.rem(z + o, 8), core)

    x_next = [spot((x + d) % 4, y, z, core) for d in (1, 3)]
    y_next = [spot(x, (y + d) % 4, z, core) for d in (1, 3)]
    twin = spot(x, y, z, 1 - core)
    greeted = [along_z(o) for o in range(1, 8)] + x_next + y_next + [twin]
    barrier = pltpu.get_barrier_semaphore()
    for peer in greeted:
        pl.semaphore_signal(barrier, inc=1, device_id=peer, device_id_type=MESH)

    for c in loads[:5]:
        c.wait()
    exps = smooth_ref[...] + scale_ref[...]
    up = jnp.left_shift(jnp.int32(1), -exps).astype(jnp.float32)
    down = jnp.left_shift(jnp.int32(1), exps + 7).astype(jnp.float32) * (2.0**-7)
    codes = jnp.floor(
        k_ref[...].astype(jnp.float32) * up[None] + off_ref[...].astype(jnp.float32) * (1.0 / 256)
    )
    coded = jnp.clip(codes, -128.0, 127.0) * down[None]
    rows[0] = coded.reshape(TOK * HEADS, DIM)
    rows[1] = v_ref[...].astype(jnp.float32).reshape(TOK * HEADS, DIM)
    for h in range(HEADS):
        for t in range(2):
            kv_send[h, t] = rows[t, pl.ds(h, TOK, stride=HEADS), :].astype(jnp.bfloat16)

    pl.semaphore_wait(barrier, len(greeted))

    far_first = (4, 3, 5, 2, 6, 1, 7)
    kv_copies = []
    for o in far_first:
        c = pltpu.make_async_remote_copy(
            kv_send.at[lax.rem(z + o, 8)], kv_all.at[core, y, x, 8 - o],
            kvs.at[o], kvr.at[8 - o], device_id=along_z(o), device_id_type=MESH,
        )
        c.start()
        kv_copies.append(c)
    kv_all[core, y, x, 0] = kv_send[z]

    loads[5].wait()
    for g in range(HEADS // 2):
        pair = q_ref[:, 16 * g : 16 * g + 16, :].astype(jnp.float32)
        for i in range(2):
            q_send[2 * g + i] = (
                pair[:, 8 * i : 8 * i + 8, :].reshape(TOK * GROUP, DIM).astype(jnp.bfloat16)
            )
    q_copies = []
    for o in far_first:
        c = pltpu.make_async_remote_copy(
            q_send.at[lax.rem(z + o, 8)], q_all.at[8 - o],
            qs.at[o], qr.at[8 - o], device_id=along_z(o), device_id_type=MESH,
        )
        c.start()
        q_copies.append(c)
    q_all[0] = q_send[z]

    for c in loads[6:]:
        c.wait()
    nth = lax.broadcasted_iota(jnp.int32, (64, BLOCKS), 0) * 4
    at_pos = lax.broadcasted_iota(jnp.int32, (64, BLOCKS), 1)
    found = jnp.zeros((64, BLOCKS), jnp.int32)
    for u in range(4):
        b = nth + u
        home = ((b >> 3) & 1) * 128 + ((b >> 1) & 3) * 32 + (b & 1) * 16 + ((b >> 4) & 1) * 8
        home = home + (((b >> 5) - z) & 7)
        here = jnp.broadcast_to(place_v[:, 32 * u : 32 * u + 1] >> 5, (64, BLOCKS))
        found = found + jnp.where(here == at_pos, home, 0)
    order_v[...] = jnp.sum(found, axis=0, keepdims=True) & (BLOCKS - 1)
    to_scalar = pltpu.make_async_copy(order_v, order, ins.at[9])
    to_scalar.start()

    def block_at(o):
        b = lax.rem(z + o, 8) * 32 + (x % 2) * 16 + core * 8 + y * 2 + x // 2
        return place_s[b // 4, (b % 4) * 32] >> 5

    channel = lax.broadcasted_iota(jnp.int32, (8, DIM), 1)
    low = jnp.full((8, DIM), 1 << 20, jnp.int32)
    high = low
    end = jnp.int32(0)
    for d in range(DOCS):
        low = jnp.where(channel == d, end, low)
        end = end + docs_s[d]
        high = jnp.where(channel == d, end, high)
    low, high = low[:1], high[:1]
    step = lax.broadcasted_iota(jnp.int32, (N_ROWS, DIM), 0)

    def key_docs(i, carry):
        pos = step + (i - REACH * TOK // N_ROWS) * N_ROWS
        at = pl.ds(i * 8, 8)
        mask = jnp.where((pos >= low) & (pos < high), 0.0, -BIG).astype(jnp.bfloat16)
        keys[at, :, pl.ds(DIM, DIM)] = mask.reshape(8, TOK, DIM)
        vals[at, :, pl.ds(DIM, DIM)] = jnp.ones((8, TOK, DIM), jnp.bfloat16)
        return carry

    lax.fori_loop(0, SORTED * TOK // N_ROWS, key_docs, 0)

    def query_docs(o, carry):
        pos = block_at(o) * TOK + step // GROUP
        q_doc[o] = jnp.where((pos >= low) & (pos < high), 1.0, 0.0).astype(jnp.bfloat16)
        return carry

    lax.fori_loop(0, 8, query_docs, 0)
    for ref in (keys, vals):
        ref[:REACH, :, :DIM] = jnp.zeros((REACH, TOK, DIM), jnp.bfloat16)
        ref[REACH + BLOCKS :, :, :DIM] = jnp.zeros((8, TOK, DIM), jnp.bfloat16)
    to_scalar.wait()

    for c in kv_copies:
        c.wait_recv()

    sends = []

    def send(ref, target):
        i = len(sends)
        c = pltpu.make_async_remote_copy(
            ref, ref, gs.at[i], gr.at[i], device_id=target, device_id_type=MESH
        )
        c.start()
        sends.append(c)
        return c

    nexts = {"x": x_next, "y": y_next}
    parts = (("x", "y", 0), ("y", "x", 4))

    def piece(rel, lo, n):
        return kv_all.at[core, (y + rel[1] + 4) % 4, (x + rel[0] + 4) % 4, pl.ds(lo, n)]

    def both(axis, rel, lo):
        return [send(piece(rel, lo, 4), target) for target in nexts[axis]]

    def moved(rel, axis, d):
        return (rel[0] + d, rel[1]) if axis == "x" else (rel[0], rel[1] + d)

    def pass_on(axis, rel, lo, copies):
        copies[0].wait_recv()
        a = send(piece(moved(rel, axis, -1), lo, 2), nexts[axis][0])
        copies[1].wait_recv()
        b = send(piece(moved(rel, axis, 1), lo + 2, 2), nexts[axis][1])
        return [a, b]

    twin_copies = []

    def line_to_twin(second, rel, lo):
        if second == "y":
            ref = kv_all.at[core, :, (x + rel[0] + 4) % 4, pl.ds(lo, 4)]
        else:
            ref = kv_all.at[core, (y + rel[1] + 4) % 4, :, pl.ds(lo, 4)]
        twin_copies.append(send(ref, twin))

    one = [both(p[0], (0, 0), p[2]) for p in parts]
    two = [(p, (0, 0), both(p[1], (0, 0), p[2])) for p in parts]
    opposite = [pass_on(p[0], (0, 0), p[2], c) for p, c in zip(parts, one)]
    for d in (-1, 1):
        for p in parts:
            rel = moved((0, 0), p[0], d)
            two.append((p, rel, both(p[1], rel, p[2])))
    last = []

    def second(entry):
        p, rel, copies = entry
        last.append((p, rel, pass_on(p[1], rel, p[2], copies)))

    def finish(entry):
        p, rel, copies = entry
        for c in copies:
            c.wait_recv()
        line_to_twin(p[1], rel, p[2])

    second(two[0])
    second(two[1])
    for p, copies in zip(parts, opposite):
        for c in copies:
            c.wait_recv()
        rel = moved((0, 0), p[0], 2)
        two.append((p, rel, both(p[1], rel, p[2])))
    for i in range(2, len(two)):
        second(two[i])
        finish(last[i - 2])
    for entry in last[len(two) - 2 :]:
        finish(entry)
    for c in twin_copies:
        c.wait_recv()
    for c in q_copies:
        c.wait_recv()

    def sort(i, carry):
        for u in range(16):
            p = i * 16 + u
            b = order[0, p]
            spot_of = (b >> 7, (b >> 5) & 3, (b >> 3) & 3, b & 7)
            keys[p + REACH, :, pl.ds(0, DIM)] = kv_all[*spot_of, 0]
            vals[p + REACH, :, pl.ds(0, DIM)] = kv_all[*spot_of, 1]
        return carry

    lax.fori_loop(0, BLOCKS // 16, sort, 0)

    lane = lax.broadcasted_iota(jnp.int32, (N_ROWS, DIM), 1)
    causal = lane <= step // GROUP

    def attend(j, carry):
        half, odd = j // 2, j % 2
        o = 4 + half - odd * (1 + 2 * half)
        start = block_at(o)

        def window(ref, c0, width):
            blocks = ref[pl.ds(start + c0 // TOK, width // TOK)]
            return blocks.reshape(width, 2 * DIM)

        q = jnp.concatenate([q_all[o], q_doc[o]], axis=1)
        top = jnp.full((N_ROWS, DIM), LOW, jnp.float32)
        for c0 in range(0, PAD, CHUNK):
            width = min(CHUNK, PAD - c0)
            s = lax.dot_general(
                q, window(keys, c0, width), (((1,), (1,)), ((), ())),
                preferred_element_type=jnp.float32,
            )
            for t in range(0, width, DIM):
                tile = s[:, t : t + DIM]
                if c0 + t == REACH * TOK:
                    tile = jnp.where(causal, tile, LOW)
                scores[:, c0 + t : c0 + t + DIM] = tile
                top = jnp.maximum(top, tile)
        peak = jnp.broadcast_to(jnp.max(top, axis=1, keepdims=True), (N_ROWS, DIM))
        total = jnp.zeros((N_ROWS, 2 * DIM), jnp.float32)
        for c0 in range(0, PAD, CHUNK):
            width = min(CHUNK, PAD - c0)
            tiles = [
                jnp.exp2((scores[:, c0 + t : c0 + t + DIM] - peak) * FACTOR).astype(jnp.bfloat16)
                for t in range(0, width, DIM)
            ]
            w = jnp.concatenate(tiles, axis=1)
            total = total + jnp.dot(
                w, window(vals, c0, width), preferred_element_type=jnp.float32
            )
        result = (total[:, :DIM] / total[:, DIM:]).astype(jnp.bfloat16)
        o_send[o] = result

        @pl.when(j < 7)
        def _():
            pltpu.make_async_remote_copy(
                o_send.at[o], o_all.at[z], os.at[o], orr.at[lax.rem(8 - o, 8)],
                device_id=along_z(o), device_id_type=MESH,
            ).start()

        return carry

    lax.fori_loop(0, 8, attend, 0)
    o_all[z] = o_send[0]
    for o in far_first:
        pltpu.make_async_remote_copy(
            o_send.at[o], o_all.at[z], os.at[o], orr.at[8 - o],
            device_id=along_z(o), device_id_type=MESH,
        ).wait_recv()
    for g in range(HEADS // 2):
        pair = [
            o_all[2 * g + i].astype(jnp.float32).reshape(TOK, GROUP, DIM) for i in range(2)
        ]
        out_ref[:, 16 * g : 16 * g + 16, :] = jnp.concatenate(pair, axis=1).astype(jnp.bfloat16)
    for c in kv_copies + q_copies + sends:
        c.wait_send()
    for o in far_first:
        pltpu.make_async_remote_copy(
            o_send.at[o], o_all.at[z], os.at[o], orr.at[8 - o],
            device_id=along_z(o), device_id_type=MESH,
        ).wait_send()


def shards(queries, keys, values, offsets, smooth_exp, scale_exp, placement, doc_lengths):
    bf, f32 = jnp.bfloat16, jnp.float32
    dma = pltpu.SemaphoreType.DMA
    hbm = pl.BlockSpec(memory_space=pltpu.HBM)
    return pl.pallas_call(
        kernel,
        out_shape=pltpu.VMEM(queries.shape, bf),
        in_specs=[hbm] * 8,
        out_specs=pl.BlockSpec(memory_space=pltpu.VMEM),
        scratch_shapes=[
            pltpu.VMEM((64, DIM), jnp.int32),
            pltpu.SMEM((64, DIM), jnp.int32),
            pltpu.SMEM((DOCS,), jnp.int32),
            pltpu.VMEM(queries.shape, bf),
            pltpu.VMEM(keys.shape, bf),
            pltpu.VMEM(values.shape, bf),
            pltpu.VMEM(offsets.shape, jnp.int32),
            pltpu.VMEM((HEADS, DIM), jnp.int32),
            pltpu.VMEM((HEADS, DIM), jnp.int32),
            pltpu.VMEM((1, BLOCKS), jnp.int32),
            pltpu.SMEM((1, BLOCKS), jnp.int32),
            pltpu.VMEM((2, TOK * HEADS, DIM), f32),
            pltpu.VMEM((HEADS, 2, TOK, DIM), bf),
            pltpu.VMEM((2, 4, 4, 8, 2, TOK, DIM), bf),
            pltpu.VMEM((HEADS, N_ROWS, DIM), bf),
            pltpu.VMEM((8, N_ROWS, DIM), bf),
            pltpu.VMEM((8, N_ROWS, DIM), bf),
            pltpu.VMEM((8, N_ROWS, DIM), bf),
            pltpu.VMEM((HEADS, N_ROWS, DIM), bf),
            pltpu.VMEM((SORTED, TOK, 2 * DIM), bf),
            pltpu.VMEM((SORTED, TOK, 2 * DIM), bf),
            pltpu.VMEM((N_ROWS, PAD), f32),
            dma((8,)), dma((8,)), dma((8,)), dma((8,)), dma((8,)), dma((8,)),
            dma((48,)), dma((48,)), dma((10,)),
        ],
        compiler_params=pltpu.CompilerParams(
            collective_id=0, has_side_effects=True, vmem_limit_bytes=60 * 2**20
        ),
        name="attend",
    )(
        placement.reshape(64, DIM), doc_lengths, queries, keys, values, offsets, smooth_exp,
        scale_exp,
    )


def solution(mesh):
    tokens = P(("ctx", "kv"), None, None)
    return jax.shard_map(
        shards,
        mesh=mesh,
        in_specs=(tokens,) * 4 + (P(),) * 4,
        out_specs=tokens,
        check_vma=False,
    )
```

```python
import jax
import jax.numpy as jnp
from jax import lax
from jax.experimental import pallas as pl
from jax.experimental.pallas import tpu as pltpu
from jax.sharding import PartitionSpec as P

MESH = pl.DeviceIdType.MESH
TOK = 32
HEADS = 8
GROUP = 8
DIM = 128
BLOCKS = 256
REACH = 64
PAD = 2176
CHUNK = 256
N_ROWS = TOK * GROUP
SORTED = REACH + BLOCKS + 8
DOCS = 16
BIG = 65536.0
FACTOR = DIM**-0.5 * 1.4426950408889634
LOW = -1e30


def spot(x, y, z, core):
    return (y * 2 + x // 2, z * 4 + (x % 2) * 2 + core)


def kernel(
    place_hbm, docs_hbm, q_hbm, k_hbm, v_hbm, off_hbm, smooth_hbm, scale_hbm, out_ref,
    place_v, place_s, docs_s, q_ref, k_ref, v_ref, off_ref, smooth_ref, scale_ref, order_v, order,
    rows, kv_send, kv_all, q_send, q_all, q_doc, o_send, o_all, keys, vals, scores, peaks,
    kvs, kvr, qs, qr, os, orr, gs, gr, ins,
):
    loads = []
    pairs = (
        (k_hbm, k_ref), (off_hbm, off_ref), (smooth_hbm, smooth_ref), (scale_hbm, scale_ref),
        (v_hbm, v_ref), (q_hbm, q_ref), (docs_hbm, docs_s), (place_hbm, place_v),
        (place_hbm, place_s),
    )
    for i, (src, dst) in enumerate(pairs):
        c = pltpu.make_async_copy(src, dst, ins.at[i])
        c.start()
        loads.append(c)
    kv = lax.axis_index("kv")
    ctx = lax.axis_index("ctx")
    y, z, core = kv // 2, ctx // 4, ctx % 2
    x = (kv % 2) * 2 + (ctx // 2) % 2

    def along_z(o):
        return spot(x, y, lax.rem(z + o, 8), core)

    along_x = [spot((x + d) % 4, y, z, core) for d in range(4)]
    along_y = [spot(x, (y + d) % 4, z, core) for d in range(4)]
    twin = spot(x, y, z, 1 - core)
    greeted = [along_z(o) for o in range(1, 8)] + along_x[1:] + along_y[1:] + [twin]
    barrier = pltpu.get_barrier_semaphore()
    for peer in greeted:
        pl.semaphore_signal(barrier, inc=1, device_id=peer, device_id_type=MESH)

    for c in loads[:5]:
        c.wait()
    exps = smooth_ref[...] + scale_ref[...]
    up = jnp.left_shift(jnp.int32(1), -exps).astype(jnp.float32)
    down = jnp.left_shift(jnp.int32(1), exps + 7).astype(jnp.float32) * (2.0**-7)
    codes = jnp.floor(
        k_ref[...].astype(jnp.float32) * up[None] + off_ref[...].astype(jnp.float32) * (1.0 / 256)
    )
    coded = jnp.clip(codes, -128.0, 127.0) * down[None]
    rows[0] = coded.reshape(TOK * HEADS, DIM)
    rows[1] = v_ref[...].astype(jnp.float32).reshape(TOK * HEADS, DIM)
    for h in range(HEADS):
        for t in range(2):
            kv_send[h, t] = rows[t, pl.ds(h, TOK, stride=HEADS), :].astype(jnp.bfloat16)

    pl.semaphore_wait(barrier, len(greeted))

    line, other = (y, x), (x, y)
    far_first = (4, 3, 5, 2, 6, 1, 7)
    kv_copies = []
    for o in far_first:
        c = pltpu.make_async_remote_copy(
            kv_send.at[lax.rem(z + o, 8)],
            kv_all.at[(8 - o) // 4, core, line[(8 - o) // 4], 0, (8 - o) % 4],
            kvs.at[o], kvr.at[8 - o], device_id=along_z(o), device_id_type=MESH,
        )
        c.start()
        kv_copies.append(c)
    kv_all[0, core, y, 0, 0] = kv_send[z]

    loads[5].wait()
    for g in range(HEADS // 2):
        pair = q_ref[:, 16 * g : 16 * g + 16, :].astype(jnp.float32)
        for i in range(2):
            q_send[2 * g + i] = (
                pair[:, 8 * i : 8 * i + 8, :].reshape(TOK * GROUP, DIM).astype(jnp.bfloat16)
            )
    q_copies = []
    for o in far_first:
        c = pltpu.make_async_remote_copy(
            q_send.at[lax.rem(z + o, 8)], q_all.at[8 - o],
            qs.at[o], qr.at[8 - o], device_id=along_z(o), device_id_type=MESH,
        )
        c.start()
        q_copies.append(c)
    q_all[0] = q_send[z]

    for c in loads[6:]:
        c.wait()
    nth = lax.broadcasted_iota(jnp.int32, (64, BLOCKS), 0) * 4
    at_pos = lax.broadcasted_iota(jnp.int32, (64, BLOCKS), 1)
    found = jnp.zeros((64, BLOCKS), jnp.int32)
    for u in range(4):
        b = nth + u
        their_x, their_y = (b & 1) * 2 + ((b >> 4) & 1), (b >> 1) & 3
        deep = ((b >> 5) - z) & 7
        first = their_y * 16 + ((their_x - x) & 3) * 4 + deep
        second = their_x * 16 + ((their_y - y) & 3) * 4 + deep + 124
        home = ((b >> 3) & 1) * 64 + jnp.where(deep < 4, first, second)
        here = jnp.broadcast_to(place_v[:, 32 * u : 32 * u + 1] >> 5, (64, BLOCKS))
        found = found + jnp.where(here == at_pos, home, 0)
    order_v[...] = jnp.sum(found, axis=0, keepdims=True) & (BLOCKS - 1)
    to_scalar = pltpu.make_async_copy(order_v, order, ins.at[9])
    to_scalar.start()

    def block_at(o):
        b = lax.rem(z + o, 8) * 32 + (x % 2) * 16 + core * 8 + y * 2 + x // 2
        return place_s[b // 4, (b % 4) * 32] >> 5

    channel = lax.broadcasted_iota(jnp.int32, (8, DIM), 1)
    low = jnp.full((8, DIM), 1 << 20, jnp.int32)
    high = low
    end = jnp.int32(0)
    for d in range(DOCS):
        low = jnp.where(channel == d, end, low)
        end = end + docs_s[d]
        high = jnp.where(channel == d, end, high)
    low, high = low[:1], high[:1]
    step = lax.broadcasted_iota(jnp.int32, (N_ROWS, DIM), 0)

    def key_docs(i, carry):
        pos = step + (i - REACH * TOK // N_ROWS) * N_ROWS
        at = pl.ds(i * 8, 8)
        mask = jnp.where((pos >= low) & (pos < high), 0.0, -BIG).astype(jnp.bfloat16)
        keys[at, :, pl.ds(DIM, DIM)] = mask.reshape(8, TOK, DIM)
        vals[at, :, pl.ds(DIM, DIM)] = jnp.ones((8, TOK, DIM), jnp.bfloat16)
        return carry

    lax.fori_loop(0, SORTED * TOK // N_ROWS, key_docs, 0)

    def query_docs(o, carry):
        pos = block_at(o) * TOK + step // GROUP
        q_doc[o] = jnp.where((pos >= low) & (pos < high), 1.0, 0.0).astype(jnp.bfloat16)
        return carry

    lax.fori_loop(0, 8, query_docs, 0)
    for ref in (keys, vals):
        ref[:REACH, :, :DIM] = jnp.zeros((REACH, TOK, DIM), jnp.bfloat16)
        ref[REACH + BLOCKS :, :, :DIM] = jnp.zeros((8, TOK, DIM), jnp.bfloat16)
    to_scalar.wait()

    sends = []

    def send(src, dst, target):
        i = len(sends)
        c = pltpu.make_async_remote_copy(
            src, dst, gs.at[i], gr.at[i], device_id=target, device_id_type=MESH
        )
        c.start()
        sends.append(c)
        return c

    arrived = dict(zip(far_first, kv_copies))
    inner, outer = (along_x, along_y), (along_y, along_x)
    own, others, whole = pl.ds(0, 1), pl.ds(1, 3), pl.ds(0, 4)

    def row(p, d, columns, depth=whole):
        return kv_all.at[p, core, (line[p] + d) % 4, columns, depth]

    def same(ref, target):
        return send(ref, ref, target)

    def spread(p, columns):
        return [same(row(p, 0, columns), outer[p][d]) for d in (1, 3)]

    def pass_on(p, columns, copies):
        copies[0].wait_recv()
        a = same(row(p, 3, columns, pl.ds(0, 2)), outer[p][1])
        copies[1].wait_recv()
        b = same(row(p, 1, columns, pl.ds(2, 2)), outer[p][3])
        return [a, b]

    def to_twin(p, d):
        return same(row(p, d, whole), twin)

    rows_in, own_in, others_in, twin_in = [], [], [], []
    for p in range(2):
        for o in far_first:
            if (8 - o) // 4 == p:
                arrived[o].wait_recv()
        rows_in.append(
            [
                send(row(p, 0, own), kv_all.at[p, core, line[p], pl.ds(4 - d, 1)], inner[p][d])
                for d in (2, 1, 3)
            ]
        )
    for p in range(2):
        own_in.append(spread(p, own))
    for p in range(2):
        for c in rows_in[p]:
            c.wait_recv()
        others_in.append(spread(p, others))
        twin_in.append(to_twin(p, 0))
    last = [pass_on(p, own, own_in[p]) for p in range(2)]
    for p in range(2):
        last[p] = last[p] + pass_on(p, others, others_in[p])
        twin_in.append(to_twin(p, 3))
        twin_in.append(to_twin(p, 1))
    for p in range(2):
        for c in last[p]:
            c.wait_recv()
        twin_in.append(to_twin(p, 2))
    for c in twin_in:
        c.wait_recv()
    for c in q_copies:
        c.wait_recv()

    def sort(i, carry):
        for u in range(16):
            p = i * 16 + u
            b = order[0, p]
            spot_of = (b >> 7, (b >> 6) & 1, (b >> 4) & 3, (b >> 2) & 3, b & 3)
            keys[p + REACH, :, pl.ds(0, DIM)] = kv_all[*spot_of, 0]
            vals[p + REACH, :, pl.ds(0, DIM)] = kv_all[*spot_of, 1]
        return carry

    lax.fori_loop(0, BLOCKS // 16, sort, 0)

    lane = lax.broadcasted_iota(jnp.int32, (N_ROWS, DIM), 1)
    causal = lane <= step // GROUP

    def window(ref, o, c0, width):
        blocks = ref[pl.ds(block_at(o) + c0 // TOK, width // TOK)]
        return blocks.reshape(width, 2 * DIM)

    def score(o, slot):
        q = jnp.concatenate([q_all[o], q_doc[o]], axis=1)
        top = jnp.full((N_ROWS, DIM), LOW, jnp.float32)
        for c0 in range(0, PAD, CHUNK):
            width = min(CHUNK, PAD - c0)
            s = lax.dot_general(
                q, window(keys, o, c0, width), (((1,), (1,)), ((), ())),
                preferred_element_type=jnp.float32,
            )
            for t in range(0, width, DIM):
                tile = s[:, t : t + DIM]
                if c0 + t == REACH * TOK:
                    tile = jnp.where(causal, tile, LOW)
                scores[slot, :, c0 + t : c0 + t + DIM] = tile
                top = jnp.maximum(top, tile)
        peaks[slot] = jnp.broadcast_to(jnp.max(top, axis=1, keepdims=True), (N_ROWS, DIM))

    def weigh(o, slot, peak):
        total = jnp.zeros((N_ROWS, 2 * DIM), jnp.float32)
        for c0 in range(0, PAD, CHUNK):
            width = min(CHUNK, PAD - c0)
            tiles = [
                jnp.exp2((scores[slot, :, c0 + t : c0 + t + DIM] - peak) * FACTOR)
                for t in range(0, width, DIM)
            ]
            w = jnp.concatenate([tile.astype(jnp.bfloat16) for tile in tiles], axis=1)
            total = total + jnp.dot(
                w, window(vals, o, c0, width), preferred_element_type=jnp.float32
            )
        o_send[o] = (total[:, :DIM] / total[:, DIM:]).astype(jnp.bfloat16)

    def home_copy(o):
        return pltpu.make_async_remote_copy(
            o_send.at[o], o_all.at[z], os.at[o], orr.at[lax.rem(8 - o, 8)],
            device_id=along_z(o), device_id_type=MESH,
        )

    score(4, 0)

    def two(i, carry):
        peak = peaks[0]
        score(3 - i, 1)
        weigh(4 + i, 0, peak)
        home_copy(4 + i).start()
        peak = peaks[1]
        score(5 + i, 0)
        weigh(3 - i, 1, peak)
        home_copy(3 - i).start()
        return carry

    lax.fori_loop(0, 3, two, 0)
    peak = peaks[0]
    score(0, 1)
    weigh(7, 0, peak)
    home_copy(7).start()
    weigh(0, 1, peaks[1])
    o_all[z] = o_send[0]
    for o in far_first:
        home_copy(o).wait_recv()
    for g in range(HEADS // 2):
        pair = [
            o_all[2 * g + i].astype(jnp.float32).reshape(TOK, GROUP, DIM) for i in range(2)
        ]
        out_ref[:, 16 * g : 16 * g + 16, :] = jnp.concatenate(pair, axis=1).astype(jnp.bfloat16)
    for c in kv_copies + q_copies + sends:
        c.wait_send()
    for o in far_first:
        home_copy(o).wait_send()


def shards(queries, keys, values, offsets, smooth_exp, scale_exp, placement, doc_lengths):
    bf, f32 = jnp.bfloat16, jnp.float32
    dma = pltpu.SemaphoreType.DMA
    hbm = pl.BlockSpec(memory_space=pltpu.HBM)
    return pl.pallas_call(
        kernel,
        out_shape=pltpu.VMEM(queries.shape, bf),
        in_specs=[hbm] * 8,
        out_specs=pl.BlockSpec(memory_space=pltpu.VMEM),
        scratch_shapes=[
            pltpu.VMEM((64, DIM), jnp.int32),
            pltpu.SMEM((64, DIM), jnp.int32),
            pltpu.SMEM((DOCS,), jnp.int32),
            pltpu.VMEM(queries.shape, bf),
            pltpu.VMEM(keys.shape, bf),
            pltpu.VMEM(values.shape, bf),
            pltpu.VMEM(offsets.shape, jnp.int32),
            pltpu.VMEM((HEADS, DIM), jnp.int32),
            pltpu.VMEM((HEADS, DIM), jnp.int32),
            pltpu.VMEM((1, BLOCKS), jnp.int32),
            pltpu.SMEM((1, BLOCKS), jnp.int32),
            pltpu.VMEM((2, TOK * HEADS, DIM), f32),
            pltpu.VMEM((HEADS, 2, TOK, DIM), bf),
            pltpu.VMEM((2, 2, 4, 4, 4, 2, TOK, DIM), bf),
            pltpu.VMEM((HEADS, N_ROWS, DIM), bf),
            pltpu.VMEM((8, N_ROWS, DIM), bf),
            pltpu.VMEM((8, N_ROWS, DIM), bf),
            pltpu.VMEM((8, N_ROWS, DIM), bf),
            pltpu.VMEM((HEADS, N_ROWS, DIM), bf),
            pltpu.VMEM((SORTED, TOK, 2 * DIM), bf),
            pltpu.VMEM((SORTED, TOK, 2 * DIM), bf),
            pltpu.VMEM((2, N_ROWS, PAD), f32),
            pltpu.VMEM((2, N_ROWS, DIM), f32),
            dma((8,)), dma((8,)), dma((8,)), dma((8,)), dma((8,)), dma((8,)),
            dma((30,)), dma((30,)), dma((10,)),
        ],
        compiler_params=pltpu.CompilerParams(
            collective_id=0, has_side_effects=True, vmem_limit_bytes=60 * 2**20
        ),
        name="attend",
    )(
        placement.reshape(64, DIM), doc_lengths, queries, keys, values, offsets, smooth_exp,
        scale_exp,
    )


def solution(mesh):
    tokens = P(("ctx", "kv"), None, None)
    return jax.shard_map(
        shards,
        mesh=mesh,
        in_specs=(tokens,) * 4 + (P(),) * 4,
        out_specs=tokens,
        check_vma=False,
    )
```

```python
import jax
import jax.numpy as jnp
from jax import lax
from jax.experimental import pallas as pl
from jax.experimental.pallas import tpu as pltpu
from jax.sharding import PartitionSpec as P

MESH = pl.DeviceIdType.MESH
TOK = 32
HEADS = 8
GROUP = 8
DIM = 128
BLOCKS = 256
REACH = 64
PAD = 2176
CHUNK = 256
N_ROWS = TOK * GROUP
SORTED = REACH + BLOCKS + 8
DOCS = 16
BIG = 65536.0
FACTOR = DIM**-0.5 * 1.4426950408889634
LOW = -1e30


def spot(x, y, z, core):
    return (y * 2 + x // 2, z * 4 + (x % 2) * 2 + core)


def kernel(
    place_hbm, docs_hbm, q_hbm, k_hbm, v_hbm, off_hbm, smooth_hbm, scale_hbm, out_ref,
    place_v, place_s, docs_s, q_ref, k_ref, v_ref, off_ref, smooth_ref, scale_ref, order_v, order,
    rows, kv_send, kv_all, q_send, q_all, q_doc, o_send, o_all, keys, vals, scores, peaks,
    kvs, kvr, qs, qr, os, orr, gs, gr, ins,
):
    kv = lax.axis_index("kv")
    ctx = lax.axis_index("ctx")
    y, z, core = kv // 2, ctx // 4, ctx % 2
    x = (kv % 2) * 2 + (ctx // 2) % 2

    def along_z(o):
        return spot(x, y, lax.rem(z + o, 8), core)

    line = y * (1 - core) + x * core
    inner = [spot((x + d * (1 - core)) % 4, (y + d * core) % 4, z, core) for d in range(4)]
    outer = [spot((x + d * core) % 4, (y + d * (1 - core)) % 4, z, core) for d in range(4)]
    twin = spot(x, y, z, 1 - core)
    greeted = [along_z(o) for o in range(1, 8)] + inner[1:] + outer[1:] + [twin]
    greeted = greeted + [spot(x, y, lax.rem(z + o, 8), 1 - core) for o in range(1, 8)]
    barrier = pltpu.get_barrier_semaphore()
    for peer in greeted:
        pl.semaphore_signal(barrier, inc=1, device_id=peer, device_id_type=MESH)

    loads = []
    pairs = (
        (k_hbm, k_ref), (off_hbm, off_ref), (smooth_hbm, smooth_ref), (scale_hbm, scale_ref),
        (v_hbm, v_ref), (q_hbm, q_ref), (docs_hbm, docs_s), (place_hbm, place_v),
        (place_hbm, place_s),
    )
    for i, (src, dst) in enumerate(pairs):
        c = pltpu.make_async_copy(src, dst, ins.at[i])
        c.start()
        loads.append(c)
    for c in loads[:5]:
        c.wait()
    exps = smooth_ref[...] + scale_ref[...]
    up = jnp.left_shift(jnp.int32(1), -exps).astype(jnp.float32)
    down = jnp.left_shift(jnp.int32(1), exps + 7).astype(jnp.float32) * (2.0**-7)
    codes = jnp.floor(
        k_ref[...].astype(jnp.float32) * up[None] + off_ref[...].astype(jnp.float32) * (1.0 / 256)
    )
    coded = jnp.clip(codes, -128.0, 127.0) * down[None]
    rows[0] = coded.reshape(TOK * HEADS, DIM)
    rows[1] = v_ref[...].astype(jnp.float32).reshape(TOK * HEADS, DIM)
    for h in range(HEADS):
        for t in range(2):
            kv_send[h, t] = rows[t, pl.ds(h, TOK, stride=HEADS), :].astype(jnp.bfloat16)

    pl.semaphore_wait(barrier, len(greeted))

    far_first = (4, 3, 5, 2, 6, 1, 7)
    kv_copies = {}
    for o in (7, 1, 6, 2, 5, 3, 4):
        to, n = (1, o - 1) if o < 5 else (0, 8 - o)
        there = y if to == 0 else x
        c = pltpu.make_async_remote_copy(
            kv_send.at[lax.rem(z + o, 8)], kv_all.at[to, there, 0, n, core],
            kvs.at[o], kvr.at[n, core],
            device_id=spot(x, y, lax.rem(z + o, 8), to), device_id_type=MESH,
        )
        c.start()
        kv_copies[o] = c
    beside = pltpu.make_async_remote_copy(
        kv_send.at[z], kv_all.at[0, y, 0, 0, 1], kvs.at[0], kvr.at[0, 1],
        device_id=twin, device_id_type=MESH,
    )

    @pl.when(core == 0)
    def _():
        kv_all[0, y, 0, 0, 0] = kv_send[z]

    @pl.when(core == 1)
    def _():
        beside.start()

    loads[5].wait()
    for g in range(HEADS // 2):
        pair = q_ref[:, 16 * g : 16 * g + 16, :].astype(jnp.float32)
        for i in range(2):
            q_send[2 * g + i] = (
                pair[:, 8 * i : 8 * i + 8, :].reshape(TOK * GROUP, DIM).astype(jnp.bfloat16)
            )
    q_all[0] = q_send[z]

    for c in loads[6:]:
        c.wait()
    nth = lax.broadcasted_iota(jnp.int32, (64, BLOCKS), 0) * 4
    at_pos = lax.broadcasted_iota(jnp.int32, (64, BLOCKS), 1)
    found = jnp.zeros((64, BLOCKS), jnp.int32)
    for u in range(4):
        b = nth + u
        their_x, their_y = (b & 1) * 2 + ((b >> 4) & 1), (b >> 1) & 3
        deep = ((b >> 5) - z) & 7
        first = (their_y * 4 + ((their_x - x) & 3)) * 4 + deep
        second = (their_x * 4 + ((their_y - y) & 3)) * 4 + 71 - deep
        home = jnp.where(deep < 4, first, second) * 2 + ((b >> 3) & 1)
        here = jnp.broadcast_to(place_v[:, 32 * u : 32 * u + 1] >> 5, (64, BLOCKS))
        found = found + jnp.where(here == at_pos, home, 0)
    order_v[...] = jnp.sum(found, axis=0, keepdims=True) & (BLOCKS - 1)
    to_scalar = pltpu.make_async_copy(order_v, order, ins.at[9])
    to_scalar.start()

    def block_at(o):
        b = lax.rem(z + o, 8) * 32 + (x % 2) * 16 + core * 8 + y * 2 + x // 2
        return place_s[b // 4, (b % 4) * 32] >> 5

    channel = lax.broadcasted_iota(jnp.int32, (8, DIM), 1)
    low = jnp.full((8, DIM), 1 << 20, jnp.int32)
    high = low
    end = jnp.int32(0)
    for d in range(DOCS):
        low = jnp.where(channel == d, end, low)
        end = end + docs_s[d]
        high = jnp.where(channel == d, end, high)
    low, high = low[:1], high[:1]
    step = lax.broadcasted_iota(jnp.int32, (N_ROWS, DIM), 0)

    def key_docs(i, carry):
        pos = step + (i - REACH * TOK // N_ROWS) * N_ROWS
        at = pl.ds(i * 8, 8)
        mask = jnp.where((pos >= low) & (pos < high), 0.0, -BIG).astype(jnp.bfloat16)
        keys[at, :, pl.ds(DIM, DIM)] = mask.reshape(8, TOK, DIM)
        vals[at, :, pl.ds(DIM, DIM)] = jnp.ones((8, TOK, DIM), jnp.bfloat16)
        return carry

    lax.fori_loop(0, SORTED * TOK // N_ROWS, key_docs, 0)

    def query_docs(o, carry):
        pos = block_at(o) * TOK + step // GROUP
        q_doc[o] = jnp.where((pos >= low) & (pos < high), 1.0, 0.0).astype(jnp.bfloat16)
        return carry

    lax.fori_loop(0, 8, query_docs, 0)
    for ref in (keys, vals):
        ref[:REACH, :, :DIM] = jnp.zeros((REACH, TOK, DIM), jnp.bfloat16)
        ref[REACH + BLOCKS :, :, :DIM] = jnp.zeros((8, TOK, DIM), jnp.bfloat16)
    to_scalar.wait()

    sends = []

    def send(src, dst, target):
        i = len(sends)
        c = pltpu.make_async_remote_copy(
            src, dst, gs.at[i], gr.at[i], device_id=target, device_id_type=MESH
        )
        c.start()
        sends.append(c)
        return c

    own, others, whole = (0, 1), (1, 3), (0, 4)

    def row(i, d, columns, half=None):
        ref = kv_all.at[core, (line + d) % 4, pl.ds(*columns), pl.ds(i, 1)]
        return ref if half is None else ref.at[:, :, pl.ds(half, 1)]

    def same(ref, target):
        return send(ref, ref, target)

    def spread(i, columns):
        return [same(row(i, 0, columns), outer[d]) for d in (1, 3)]

    def pass_on(i, columns, copies):
        copies[0].wait_recv()
        a = same(row(i, 3, columns, 0), outer[1])
        copies[1].wait_recv()
        b = same(row(i, 1, columns, 1), outer[3])
        return [a, b]

    def to_twin(i, d):
        return same(row(i, d, whole), twin)

    def arrive(n, c):
        return pltpu.make_async_remote_copy(
            kv_send.at[0], kv_all.at[core, line, 0, n, c], kvs.at[0], kvr.at[n, c],
            device_id=twin, device_id_type=MESH,
        )

    rows_in, twin_in, own_in = [], [], []
    for i in range(4):
        for c in range(2):
            if i or c:
                arrive(i, c).wait_recv()
            else:
                pl.when(core == 1)(arrive(i, c).wait_recv)
        rows_in.append(
            [
                send(row(i, 0, own), row(i, 0, (4 - d, 1)), inner[d])
                for d in (2, 1, 3)
            ]
        )
        own_in.append(spread(i, own))
    q_copies = []
    for o in far_first:
        c = pltpu.make_async_remote_copy(
            q_send.at[lax.rem(z + o, 8)], q_all.at[8 - o],
            qs.at[o], qr.at[8 - o], device_id=along_z(o), device_id_type=MESH,
        )
        c.start()
        q_copies.append(c)
    ring_in, last = [], []

    def widen(i):
        for c in rows_in[i]:
            c.wait_recv()
        ring_in.append(spread(i, others))
        twin_in.append(to_twin(i, 0))
        last.append([])

    def turn(i):
        last[i] += pass_on(i, others, ring_in[i])
        twin_in.append(to_twin(i, 3))
        twin_in.append(to_twin(i, 1))

    def finish(i):
        for c in last[i]:
            c.wait_recv()
        twin_in.append(to_twin(i, 2))

    for i in range(4):
        widen(i)
    for i in range(4):
        last[i] += pass_on(i, own, own_in[i])
    for i in range(4):
        turn(i)
    for i in range(4):
        finish(i)
    for c in twin_in:
        c.wait_recv()
    for c in q_copies:
        c.wait_recv()

    def sort(i, carry):
        for u in range(16):
            p = i * 16 + u
            b = order[0, p]
            spot_of = (b >> 7, (b >> 5) & 3, (b >> 3) & 3, (b >> 1) & 3, b & 1)
            keys[p + REACH, :, pl.ds(0, DIM)] = kv_all[*spot_of, 0]
            vals[p + REACH, :, pl.ds(0, DIM)] = kv_all[*spot_of, 1]
        return carry

    lax.fori_loop(0, BLOCKS // 16, sort, 0)

    lane = lax.broadcasted_iota(jnp.int32, (N_ROWS, DIM), 1)
    causal = lane <= step // GROUP

    def window(ref, o, c0, width):
        blocks = ref[pl.ds(block_at(o) + c0 // TOK, width // TOK)]
        return blocks.reshape(width, 2 * DIM)

    def score(o, slot):
        q = jnp.concatenate([q_all[o], q_doc[o]], axis=1)
        top = jnp.full((N_ROWS, DIM), LOW, jnp.float32)
        for c0 in range(0, PAD, CHUNK):
            width = min(CHUNK, PAD - c0)
            s = lax.dot_general(
                q, window(keys, o, c0, width), (((1,), (1,)), ((), ())),
                preferred_element_type=jnp.float32,
            )
            for t in range(0, width, DIM):
                tile = s[:, t : t + DIM]
                if c0 + t == REACH * TOK:
                    tile = jnp.where(causal, tile, LOW)
                scores[slot, :, c0 + t : c0 + t + DIM] = tile
                top = jnp.maximum(top, tile)
        peaks[slot] = jnp.broadcast_to(jnp.max(top, axis=1, keepdims=True), (N_ROWS, DIM))

    def weigh(o, slot, peak):
        total = jnp.zeros((N_ROWS, 2 * DIM), jnp.float32)
        for c0 in range(0, PAD, CHUNK):
            width = min(CHUNK, PAD - c0)
            tiles = [
                jnp.exp2((scores[slot, :, c0 + t : c0 + t + DIM] - peak) * FACTOR)
                for t in range(0, width, DIM)
            ]
            w = jnp.concatenate([tile.astype(jnp.bfloat16) for tile in tiles], axis=1)
            total = total + jnp.dot(
                w, window(vals, o, c0, width), preferred_element_type=jnp.float32
            )
        o_send[o] = (total[:, :DIM] / total[:, DIM:]).astype(jnp.bfloat16)

    def home_copy(o):
        return pltpu.make_async_remote_copy(
            o_send.at[o], o_all.at[z], os.at[o], orr.at[lax.rem(8 - o, 8)],
            device_id=along_z(o), device_id_type=MESH,
        )

    score(4, 0)

    def two(i, carry):
        peak = peaks[0]
        score(3 - i, 1)
        weigh(4 + i, 0, peak)
        home_copy(4 + i).start()
        peak = peaks[1]
        score(5 + i, 0)
        weigh(3 - i, 1, peak)
        home_copy(3 - i).start()
        return carry

    lax.fori_loop(0, 3, two, 0)
    peak = peaks[0]
    score(0, 1)
    weigh(7, 0, peak)
    home_copy(7).start()
    weigh(0, 1, peaks[1])
    o_all[z] = o_send[0]
    for o in far_first:
        home_copy(o).wait_recv()
    for g in range(HEADS // 2):
        pair = [
            o_all[2 * g + i].astype(jnp.float32).reshape(TOK, GROUP, DIM) for i in range(2)
        ]
        out_ref[:, 16 * g : 16 * g + 16, :] = jnp.concatenate(pair, axis=1).astype(jnp.bfloat16)
    pl.when(core == 1)(beside.wait_send)
    for c in list(kv_copies.values()) + q_copies + sends:
        c.wait_send()
    for o in far_first:
        home_copy(o).wait_send()


def shards(queries, keys, values, offsets, smooth_exp, scale_exp, placement, doc_lengths):
    bf, f32 = jnp.bfloat16, jnp.float32
    dma = pltpu.SemaphoreType.DMA
    hbm = pl.BlockSpec(memory_space=pltpu.HBM)
    return pl.pallas_call(
        kernel,
        out_shape=pltpu.VMEM(queries.shape, bf),
        in_specs=[hbm] * 8,
        out_specs=pl.BlockSpec(memory_space=pltpu.VMEM),
        scratch_shapes=[
            pltpu.VMEM((64, DIM), jnp.int32),
            pltpu.SMEM((64, DIM), jnp.int32),
            pltpu.SMEM((DOCS,), jnp.int32),
            pltpu.VMEM(queries.shape, bf),
            pltpu.VMEM(keys.shape, bf),
            pltpu.VMEM(values.shape, bf),
            pltpu.VMEM(offsets.shape, jnp.int32),
            pltpu.VMEM((HEADS, DIM), jnp.int32),
            pltpu.VMEM((HEADS, DIM), jnp.int32),
            pltpu.VMEM((1, BLOCKS), jnp.int32),
            pltpu.SMEM((1, BLOCKS), jnp.int32),
            pltpu.VMEM((2, TOK * HEADS, DIM), f32),
            pltpu.VMEM((HEADS, 2, TOK, DIM), bf),
            pltpu.VMEM((2, 4, 4, 4, 2, 2, TOK, DIM), bf),
            pltpu.VMEM((HEADS, N_ROWS, DIM), bf),
            pltpu.VMEM((8, N_ROWS, DIM), bf),
            pltpu.VMEM((8, N_ROWS, DIM), bf),
            pltpu.VMEM((8, N_ROWS, DIM), bf),
            pltpu.VMEM((HEADS, N_ROWS, DIM), bf),
            pltpu.VMEM((SORTED, TOK, 2 * DIM), bf),
            pltpu.VMEM((SORTED, TOK, 2 * DIM), bf),
            pltpu.VMEM((2, N_ROWS, PAD), f32),
            pltpu.VMEM((2, N_ROWS, DIM), f32),
            dma((8,)), dma((4, 2)), dma((8,)), dma((8,)), dma((8,)), dma((8,)),
            dma((60,)), dma((60,)), dma((10,)),
        ],
        compiler_params=pltpu.CompilerParams(
            collective_id=0, has_side_effects=True, vmem_limit_bytes=60 * 2**20
        ),
        name="attend",
    )(
        placement.reshape(64, DIM), doc_lengths, queries, keys, values, offsets, smooth_exp,
        scale_exp,
    )


def solution(mesh):
    tokens = P(("ctx", "kv"), None, None)
    return jax.shard_map(
        shards,
        mesh=mesh,
        in_specs=(tokens,) * 4 + (P(),) * 4,
        out_specs=tokens,
        check_vma=False,
    )
```

```python
import jax
import jax.numpy as jnp
from jax import lax
from jax.experimental import pallas as pl
from jax.experimental.pallas import tpu as pltpu
from jax.sharding import PartitionSpec as P

MESH = pl.DeviceIdType.MESH
TOK = 32
HEADS = 8
GROUP = 8
DIM = 128
BLOCKS = 256
REACH = 64
PAD = 2176
CHUNK = 256
N_ROWS = TOK * GROUP
SORTED = REACH + BLOCKS + 8
DOCS = 16
BIG = 65536.0
FACTOR = DIM**-0.5 * 1.4426950408889634
LOW = -1e30


def spot(x, y, z, core):
    return (y * 2 + x // 2, z * 4 + (x % 2) * 2 + core)


def kernel(
    place_hbm, docs_hbm, q_hbm, k_hbm, v_hbm, off_hbm, smooth_hbm, scale_hbm, out_ref,
    place_v, place_s, docs_s, q_ref, k_ref, v_ref, off_ref, smooth_ref, scale_ref, order_v, order,
    rows, kv_send, kv_all, q_send, q_all, q_doc, o_send, o_all, keys, vals, scores, peaks,
    kvs, kvr, qs, qr, os, orr, gs, gr, ins,
):
    kv = lax.axis_index("kv")
    ctx = lax.axis_index("ctx")
    y, z, core = kv // 2, ctx // 4, ctx % 2
    x = (kv % 2) * 2 + (ctx // 2) % 2

    def along_z(o):
        return spot(x, y, lax.rem(z + o, 8), core)

    line = y * (1 - core) + x * core
    inner = [spot((x + d * (1 - core)) % 4, (y + d * core) % 4, z, core) for d in range(4)]
    outer = [spot((x + d * core) % 4, (y + d * (1 - core)) % 4, z, core) for d in range(4)]
    twin = spot(x, y, z, 1 - core)
    greeted = [along_z(o) for o in range(1, 8)] + inner[1:] + outer[1:] + [twin]
    cross = [lax.rem(z + k * (1 - 2 * core) + 8, 8) for k in range(1, 5)]
    greeted = greeted + [spot(x, y, there, 1 - core) for there in cross]
    barrier = pltpu.get_barrier_semaphore()
    for peer in greeted:
        pl.semaphore_signal(barrier, inc=1, device_id=peer, device_id_type=MESH)

    loads = []
    pairs = (
        (k_hbm, k_ref), (off_hbm, off_ref), (smooth_hbm, smooth_ref), (scale_hbm, scale_ref),
        (v_hbm, v_ref), (q_hbm, q_ref), (docs_hbm, docs_s), (place_hbm, place_v),
        (place_hbm, place_s),
    )
    for i, (src, dst) in enumerate(pairs):
        c = pltpu.make_async_copy(src, dst, ins.at[i])
        c.start()
        loads.append(c)
    for c in loads[:5]:
        c.wait()
    exps = smooth_ref[...] + scale_ref[...]
    up = jnp.left_shift(jnp.int32(1), -exps).astype(jnp.float32)
    down = jnp.left_shift(jnp.int32(1), exps + 7).astype(jnp.float32) * (2.0**-7)
    codes = jnp.floor(
        k_ref[...].astype(jnp.float32) * up[None] + off_ref[...].astype(jnp.float32) * (1.0 / 256)
    )
    coded = jnp.clip(codes, -128.0, 127.0) * down[None]
    rows[0] = coded.reshape(TOK * HEADS, DIM)
    rows[1] = v_ref[...].astype(jnp.float32).reshape(TOK * HEADS, DIM)
    for h in range(HEADS):
        for t in range(2):
            kv_send[h, t] = rows[t, pl.ds(h, TOK, stride=HEADS), :].astype(jnp.bfloat16)

    pl.semaphore_wait(barrier, len(greeted))

    far_first = (4, 3, 5, 2, 6, 1, 7)
    kv_copies = {}
    for o in (7, 1, 6, 2, 5, 3, 4):
        to, n = (1, o - 1) if o < 5 else (0, 8 - o)
        there = y if to == 0 else x
        c = pltpu.make_async_remote_copy(
            kv_send.at[lax.rem(z + o, 8)], kv_all.at[to, there, 0, n, core],
            kvs.at[o], kvr.at[n, core],
            device_id=spot(x, y, lax.rem(z + o, 8), to), device_id_type=MESH,
        )
        c.start()
        kv_copies[o] = c
    beside = pltpu.make_async_remote_copy(
        kv_send.at[z], kv_all.at[0, y, 0, 0, 1], kvs.at[0], kvr.at[0, 1],
        device_id=twin, device_id_type=MESH,
    )

    @pl.when(core == 0)
    def _():
        kv_all[0, y, 0, 0, 0] = kv_send[z]

    @pl.when(core == 1)
    def _():
        beside.start()

    loads[5].wait()
    for g in range(HEADS // 2):
        pair = q_ref[:, 16 * g : 16 * g + 16, :].astype(jnp.float32)
        for i in range(2):
            q_send[2 * g + i] = (
                pair[:, 8 * i : 8 * i + 8, :].reshape(TOK * GROUP, DIM).astype(jnp.bfloat16)
            )
    q_all[0] = q_send[z]

    for c in loads[6:]:
        c.wait()
    nth = lax.broadcasted_iota(jnp.int32, (64, BLOCKS), 0) * 4
    at_pos = lax.broadcasted_iota(jnp.int32, (64, BLOCKS), 1)
    found = jnp.zeros((64, BLOCKS), jnp.int32)
    for u in range(4):
        b = nth + u
        their_x, their_y = (b & 1) * 2 + ((b >> 4) & 1), (b >> 1) & 3
        deep = ((b >> 5) - z) & 7
        first = (their_y * 4 + ((their_x - x) & 3)) * 4 + deep
        second = (their_x * 4 + ((their_y - y) & 3)) * 4 + 71 - deep
        home = jnp.where(deep < 4, first, second) * 2 + ((b >> 3) & 1)
        here = jnp.broadcast_to(place_v[:, 32 * u : 32 * u + 1] >> 5, (64, BLOCKS))
        found = found + jnp.where(here == at_pos, home, 0)
    order_v[...] = jnp.sum(found, axis=0, keepdims=True) & (BLOCKS - 1)
    to_scalar = pltpu.make_async_copy(order_v, order, ins.at[9])
    to_scalar.start()

    def block_at(o):
        b = lax.rem(z + o, 8) * 32 + (x % 2) * 16 + core * 8 + y * 2 + x // 2
        return place_s[b // 4, (b % 4) * 32] >> 5

    channel = lax.broadcasted_iota(jnp.int32, (8, DIM), 1)
    low = jnp.full((8, DIM), 1 << 20, jnp.int32)
    high = low
    end = jnp.int32(0)
    for d in range(DOCS):
        low = jnp.where(channel == d, end, low)
        end = end + docs_s[d]
        high = jnp.where(channel == d, end, high)
    low, high = low[:1], high[:1]
    step = lax.broadcasted_iota(jnp.int32, (N_ROWS, DIM), 0)

    def key_docs(i, carry):
        pos = step + (i - REACH * TOK // N_ROWS) * N_ROWS
        at = pl.ds(i * 8, 8)
        mask = jnp.where((pos >= low) & (pos < high), 0.0, -BIG).astype(jnp.bfloat16)
        keys[at, :, pl.ds(DIM, DIM)] = mask.reshape(8, TOK, DIM)
        vals[at, :, pl.ds(DIM, DIM)] = jnp.ones((8, TOK, DIM), jnp.bfloat16)
        return carry

    lax.fori_loop(0, SORTED * TOK // N_ROWS, key_docs, 0)

    def query_docs(o, carry):
        pos = block_at(o) * TOK + step // GROUP
        q_doc[o] = jnp.where((pos >= low) & (pos < high), 1.0, 0.0).astype(jnp.bfloat16)
        return carry

    lax.fori_loop(0, 8, query_docs, 0)
    for ref in (keys, vals):
        ref[:REACH, :, :DIM] = jnp.zeros((REACH, TOK, DIM), jnp.bfloat16)
        ref[REACH + BLOCKS :, :, :DIM] = jnp.zeros((8, TOK, DIM), jnp.bfloat16)
    to_scalar.wait()

    sends = []

    def send(src, dst, target):
        i = len(sends)
        c = pltpu.make_async_remote_copy(
            src, dst, gs.at[i], gr.at[i], device_id=target, device_id_type=MESH
        )
        c.start()
        sends.append(c)
        return c

    own, others, whole = (0, 1), (1, 3), (0, 4)

    def row(i, d, columns, half=None):
        ref = kv_all.at[core, (line + d) % 4, pl.ds(*columns), pl.ds(i, 1)]
        return ref if half is None else ref.at[:, :, pl.ds(half, 1)]

    def same(ref, target):
        return send(ref, ref, target)

    def spread(i, columns):
        return [same(row(i, 0, columns), outer[d]) for d in (1, 3)]

    def pass_on(i, columns, copies):
        copies[0].wait_recv()
        a = same(row(i, 3, columns, 0), outer[1])
        copies[1].wait_recv()
        b = same(row(i, 1, columns, 1), outer[3])
        return [a, b]

    def to_twin(i, d):
        return same(row(i, d, whole), twin)

    def arrive(n, c):
        return pltpu.make_async_remote_copy(
            kv_send.at[0], kv_all.at[core, line, 0, n, c], kvs.at[0], kvr.at[n, c],
            device_id=twin, device_id_type=MESH,
        )

    rows_in, twin_in, own_in = [], [], []
    for i in range(4):
        for c in range(2):
            if i or c:
                arrive(i, c).wait_recv()
            else:
                pl.when(core == 1)(arrive(i, c).wait_recv)
        rows_in.append(
            [
                send(row(i, 0, own), row(i, 0, (4 - d, 1)), inner[d])
                for d in (2, 1, 3)
            ]
        )
        own_in.append(spread(i, own))
    q_copies = []
    for o in far_first:
        c = pltpu.make_async_remote_copy(
            q_send.at[lax.rem(z + o, 8)], q_all.at[8 - o],
            qs.at[o], qr.at[8 - o], device_id=along_z(o), device_id_type=MESH,
        )
        c.start()
        q_copies.append(c)
    ring_in, last = [], []

    def widen(i):
        for c in rows_in[i]:
            c.wait_recv()
        ring_in.append(spread(i, others))
        twin_in.append(to_twin(i, 0))
        last.append([])

    def finish(i):
        for c in last[i]:
            c.wait_recv()
        twin_in.append(to_twin(i, 2))

    for i in range(4):
        widen(i)
    for i in range(4):
        last[i] += pass_on(i, own, own_in[i])
    for i in range(4):
        last[i] += pass_on(i, others, ring_in[i])
    for i in range(4):
        twin_in.append(to_twin(i, 3))
        twin_in.append(to_twin(i, 1))
    for i in range(4):
        finish(i)
    for c in twin_in:
        c.wait_recv()
    for c in q_copies:
        c.wait_recv()

    def sort(i, carry):
        for u in range(16):
            p = i * 16 + u
            b = order[0, p]
            spot_of = (b >> 7, (b >> 5) & 3, (b >> 3) & 3, (b >> 1) & 3, b & 1)
            keys[p + REACH, :, pl.ds(0, DIM)] = kv_all[*spot_of, 0]
            vals[p + REACH, :, pl.ds(0, DIM)] = kv_all[*spot_of, 1]
        return carry

    lax.fori_loop(0, BLOCKS // 16, sort, 0)

    lane = lax.broadcasted_iota(jnp.int32, (N_ROWS, DIM), 1)
    causal = lane <= step // GROUP

    def window(ref, o, c0, width):
        blocks = ref[pl.ds(block_at(o) + c0 // TOK, width // TOK)]
        return blocks.reshape(width, 2 * DIM)

    def score(o, slot):
        q = jnp.concatenate([q_all[o], q_doc[o]], axis=1)
        top = jnp.full((N_ROWS, DIM), LOW, jnp.float32)
        for c0 in range(0, PAD, CHUNK):
            width = min(CHUNK, PAD - c0)
            s = lax.dot_general(
                q, window(keys, o, c0, width), (((1,), (1,)), ((), ())),
                preferred_element_type=jnp.float32,
            )
            for t in range(0, width, DIM):
                tile = s[:, t : t + DIM]
                if c0 + t == REACH * TOK:
                    tile = jnp.where(causal, tile, LOW)
                scores[slot, :, c0 + t : c0 + t + DIM] = tile
                top = jnp.maximum(top, tile)
        peaks[slot] = jnp.broadcast_to(jnp.max(top, axis=1, keepdims=True), (N_ROWS, DIM))

    def weigh(o, slot, peak):
        total = jnp.zeros((N_ROWS, 2 * DIM), jnp.float32)
        for c0 in range(0, PAD, CHUNK):
            width = min(CHUNK, PAD - c0)
            tiles = [
                jnp.exp2((scores[slot, :, c0 + t : c0 + t + DIM] - peak) * FACTOR)
                for t in range(0, width, DIM)
            ]
            w = jnp.concatenate([tile.astype(jnp.bfloat16) for tile in tiles], axis=1)
            total = total + jnp.dot(
                w, window(vals, o, c0, width), preferred_element_type=jnp.float32
            )
        o_send[o] = (total[:, :DIM] / total[:, DIM:]).astype(jnp.bfloat16)

    def home_copy(o):
        return pltpu.make_async_remote_copy(
            o_send.at[o], o_all.at[z], os.at[o], orr.at[lax.rem(8 - o, 8)],
            device_id=along_z(o), device_id_type=MESH,
        )

    way = 1 - 2 * core
    score(4, 0)

    def two(i, carry):
        a, b = 4 + way * i, 4 - way * (i + 1)
        peak = peaks[0]
        score(b, 1)
        weigh(a, 0, peak)
        home_copy(a).start()
        peak = peaks[1]
        score(a + way, 0)
        weigh(b, 1, peak)
        home_copy(b).start()
        return carry

    lax.fori_loop(0, 3, two, 0)
    peak = peaks[0]
    score(0, 1)
    weigh(4 + 3 * way, 0, peak)
    home_copy(4 + 3 * way).start()
    weigh(0, 1, peaks[1])
    o_all[z] = o_send[0]
    for o in far_first:
        home_copy(o).wait_recv()
    for g in range(HEADS // 2):
        pair = [
            o_all[2 * g + i].astype(jnp.float32).reshape(TOK, GROUP, DIM) for i in range(2)
        ]
        out_ref[:, 16 * g : 16 * g + 16, :] = jnp.concatenate(pair, axis=1).astype(jnp.bfloat16)
    pl.when(core == 1)(beside.wait_send)
    for c in list(kv_copies.values()) + q_copies + sends:
        c.wait_send()
    for o in far_first:
        home_copy(o).wait_send()


def shards(queries, keys, values, offsets, smooth_exp, scale_exp, placement, doc_lengths):
    bf, f32 = jnp.bfloat16, jnp.float32
    dma = pltpu.SemaphoreType.DMA
    hbm = pl.BlockSpec(memory_space=pltpu.HBM)
    return pl.pallas_call(
        kernel,
        out_shape=pltpu.VMEM(queries.shape, bf),
        in_specs=[hbm] * 8,
        out_specs=pl.BlockSpec(memory_space=pltpu.VMEM),
        scratch_shapes=[
            pltpu.VMEM((64, DIM), jnp.int32),
            pltpu.SMEM((64, DIM), jnp.int32),
            pltpu.SMEM((DOCS,), jnp.int32),
            pltpu.VMEM(queries.shape, bf),
            pltpu.VMEM(keys.shape, bf),
            pltpu.VMEM(values.shape, bf),
            pltpu.VMEM(offsets.shape, jnp.int32),
            pltpu.VMEM((HEADS, DIM), jnp.int32),
            pltpu.VMEM((HEADS, DIM), jnp.int32),
            pltpu.VMEM((1, BLOCKS), jnp.int32),
            pltpu.SMEM((1, BLOCKS), jnp.int32),
            pltpu.VMEM((2, TOK * HEADS, DIM), f32),
            pltpu.VMEM((HEADS, 2, TOK, DIM), bf),
            pltpu.VMEM((2, 4, 4, 4, 2, 2, TOK, DIM), bf),
            pltpu.VMEM((HEADS, N_ROWS, DIM), bf),
            pltpu.VMEM((8, N_ROWS, DIM), bf),
            pltpu.VMEM((8, N_ROWS, DIM), bf),
            pltpu.VMEM((8, N_ROWS, DIM), bf),
            pltpu.VMEM((HEADS, N_ROWS, DIM), bf),
            pltpu.VMEM((SORTED, TOK, 2 * DIM), bf),
            pltpu.VMEM((SORTED, TOK, 2 * DIM), bf),
            pltpu.VMEM((2, N_ROWS, PAD), f32),
            pltpu.VMEM((2, N_ROWS, DIM), f32),
            dma((8,)), dma((4, 2)), dma((8,)), dma((8,)), dma((8,)), dma((8,)),
            dma((60,)), dma((60,)), dma((10,)),
        ],
        compiler_params=pltpu.CompilerParams(
            collective_id=0, has_side_effects=True, vmem_limit_bytes=60 * 2**20
        ),
        name="attend",
    )(
        placement.reshape(64, DIM), doc_lengths, queries, keys, values, offsets, smooth_exp,
        scale_exp,
    )


def solution(mesh):
    tokens = P(("ctx", "kv"), None, None)
    return jax.shard_map(
        shards,
        mesh=mesh,
        in_specs=(tokens,) * 4 + (P(),) * 4,
        out_specs=tokens,
        check_vma=False,
    )
```

```python
import jax
import jax.numpy as jnp
from jax import lax
from jax.experimental import pallas as pl
from jax.experimental.pallas import tpu as pltpu
from jax.sharding import PartitionSpec as P

MESH = pl.DeviceIdType.MESH
TOK = 32
HEADS = 8
GROUP = 8
DIM = 128
BLOCKS = 256
REACH = 64
PAD = 2176
CHUNK = 256
N_ROWS = TOK * GROUP
SORTED = REACH + BLOCKS + 8
DOCS = 16
BIG = 65536.0
HALF = N_ROWS // 2
FACTOR = DIM**-0.5 * 1.4426950408889634
LOW = -1e30


def spot(x, y, z, core):
    return (y * 2 + x // 2, z * 4 + (x % 2) * 2 + core)


def kernel(
    place_hbm, docs_hbm, q_hbm, k_hbm, v_hbm, off_hbm, smooth_hbm, scale_hbm, out_ref,
    place_v, place_s, docs_s, q_ref, k_ref, v_ref, off_ref, smooth_ref, scale_ref, order_v, order,
    rows, kv_send, kv_all, q_send, q_all, q_doc, o_send, o_all, keys, vals, scores, peaks,
    kvs, kvr, qs, qr, os, orr, gs, gr, ins,
):
    kv = lax.axis_index("kv")
    ctx = lax.axis_index("ctx")
    y, z, core = kv // 2, ctx // 4, ctx % 2
    x = (kv % 2) * 2 + (ctx // 2) % 2

    def along_z(o):
        return spot(x, y, lax.rem(z + o, 8), core)

    line = y * (1 - core) + x * core
    inner = [spot((x + d * (1 - core)) % 4, (y + d * core) % 4, z, core) for d in range(4)]
    outer = [spot((x + d * core) % 4, (y + d * (1 - core)) % 4, z, core) for d in range(4)]
    twin = spot(x, y, z, 1 - core)
    greeted = [along_z(o) for o in range(1, 8)] + inner[1:] + outer[1:] + [twin]
    greeted = greeted + [spot(x, y, lax.rem(z + o, 8), 1 - core) for o in range(1, 8)]
    barrier = pltpu.get_barrier_semaphore()
    for peer in greeted:
        pl.semaphore_signal(barrier, inc=1, device_id=peer, device_id_type=MESH)

    loads = []
    pairs = (
        (k_hbm, k_ref), (off_hbm, off_ref), (smooth_hbm, smooth_ref), (scale_hbm, scale_ref),
        (v_hbm, v_ref), (q_hbm, q_ref), (docs_hbm, docs_s), (place_hbm, place_v),
        (place_hbm, place_s),
    )
    for i, (src, dst) in enumerate(pairs):
        c = pltpu.make_async_copy(src, dst, ins.at[i])
        c.start()
        loads.append(c)
    for c in loads[:5]:
        c.wait()
    exps = smooth_ref[...] + scale_ref[...]
    up = jnp.left_shift(jnp.int32(1), -exps).astype(jnp.float32)
    down = jnp.left_shift(jnp.int32(1), exps + 7).astype(jnp.float32) * (2.0**-7)
    codes = jnp.floor(
        k_ref[...].astype(jnp.float32) * up[None] + off_ref[...].astype(jnp.float32) * (1.0 / 256)
    )
    coded = jnp.clip(codes, -128.0, 127.0) * down[None]
    rows[0] = coded.reshape(TOK * HEADS, DIM)
    rows[1] = v_ref[...].astype(jnp.float32).reshape(TOK * HEADS, DIM)
    for h in range(HEADS):
        for t in range(2):
            kv_send[h, t] = rows[t, pl.ds(h, TOK, stride=HEADS), :].astype(jnp.bfloat16)

    pl.semaphore_wait(barrier, len(greeted))

    far_first = (4, 3, 5, 2, 6, 1, 7)
    kv_copies = {}
    for o in (7, 1, 6, 2, 5, 3, 4):
        to, n = (1, o - 1) if o < 5 else (0, 8 - o)
        there = y if to == 0 else x
        c = pltpu.make_async_remote_copy(
            kv_send.at[lax.rem(z + o, 8)], kv_all.at[to, there, 0, n, core],
            kvs.at[o], kvr.at[n, core],
            device_id=spot(x, y, lax.rem(z + o, 8), to), device_id_type=MESH,
        )
        c.start()
        kv_copies[o] = c
    beside = pltpu.make_async_remote_copy(
        kv_send.at[z], kv_all.at[0, y, 0, 0, 1], kvs.at[0], kvr.at[0, 1],
        device_id=twin, device_id_type=MESH,
    )

    @pl.when(core == 0)
    def _():
        kv_all[0, y, 0, 0, 0] = kv_send[z]

    @pl.when(core == 1)
    def _():
        beside.start()

    loads[5].wait()
    for g in range(HEADS // 2):
        pair = q_ref[:, 16 * g : 16 * g + 16, :].astype(jnp.float32)
        for i in range(2):
            q_send[2 * g + i] = (
                pair[:, 8 * i : 8 * i + 8, :].reshape(TOK * GROUP, DIM).astype(jnp.bfloat16)
            )
    q_all[0] = q_send[z]

    for c in loads[6:]:
        c.wait()
    nth = lax.broadcasted_iota(jnp.int32, (64, BLOCKS), 0) * 4
    at_pos = lax.broadcasted_iota(jnp.int32, (64, BLOCKS), 1)
    found = jnp.zeros((64, BLOCKS), jnp.int32)
    for u in range(4):
        b = nth + u
        their_x, their_y = (b & 1) * 2 + ((b >> 4) & 1), (b >> 1) & 3
        deep = ((b >> 5) - z) & 7
        first = (their_y * 4 + ((their_x - x) & 3)) * 4 + deep
        second = (their_x * 4 + ((their_y - y) & 3)) * 4 + 71 - deep
        home = jnp.where(deep < 4, first, second) * 2 + ((b >> 3) & 1)
        here = jnp.broadcast_to(place_v[:, 32 * u : 32 * u + 1] >> 5, (64, BLOCKS))
        found = found + jnp.where(here == at_pos, home, 0)
    order_v[...] = jnp.sum(found, axis=0, keepdims=True) & (BLOCKS - 1)
    to_scalar = pltpu.make_async_copy(order_v, order, ins.at[9])
    to_scalar.start()

    def block_at(o):
        b = lax.rem(z + o, 8) * 32 + (x % 2) * 16 + core * 8 + y * 2 + x // 2
        return place_s[b // 4, (b % 4) * 32] >> 5

    channel = lax.broadcasted_iota(jnp.int32, (8, DIM), 1)
    low = jnp.full((8, DIM), 1 << 20, jnp.int32)
    high = low
    end = jnp.int32(0)
    for d in range(DOCS):
        low = jnp.where(channel == d, end, low)
        end = end + docs_s[d]
        high = jnp.where(channel == d, end, high)
    low, high = low[:1], high[:1]
    step = lax.broadcasted_iota(jnp.int32, (N_ROWS, DIM), 0)

    def key_docs(i, carry):
        pos = step + (i - REACH * TOK // N_ROWS) * N_ROWS
        at = pl.ds(i * 8, 8)
        mask = jnp.where((pos >= low) & (pos < high), 0.0, -BIG).astype(jnp.bfloat16)
        keys[at, :, pl.ds(DIM, DIM)] = mask.reshape(8, TOK, DIM)
        vals[at, :, pl.ds(DIM, DIM)] = jnp.ones((8, TOK, DIM), jnp.bfloat16)
        return carry

    lax.fori_loop(0, SORTED * TOK // N_ROWS, key_docs, 0)

    def query_docs(o, carry):
        pos = block_at(o) * TOK + step // GROUP
        q_doc[o] = jnp.where((pos >= low) & (pos < high), 1.0, 0.0).astype(jnp.bfloat16)
        return carry

    lax.fori_loop(0, 8, query_docs, 0)
    for ref in (keys, vals):
        ref[:REACH, :, :DIM] = jnp.zeros((REACH, TOK, DIM), jnp.bfloat16)
        ref[REACH + BLOCKS :, :, :DIM] = jnp.zeros((8, TOK, DIM), jnp.bfloat16)
    to_scalar.wait()

    sends = []

    def send(src, dst, target):
        i = len(sends)
        c = pltpu.make_async_remote_copy(
            src, dst, gs.at[i], gr.at[i], device_id=target, device_id_type=MESH
        )
        c.start()
        sends.append(c)
        return c

    own, others, whole = (0, 1), (1, 3), (0, 4)

    def row(i, d, columns, half=None):
        ref = kv_all.at[core, (line + d) % 4, pl.ds(*columns), pl.ds(i, 1)]
        return ref if half is None else ref.at[:, :, pl.ds(half, 1)]

    def same(ref, target):
        return send(ref, ref, target)

    def spread(i, columns):
        return [same(row(i, 0, columns), outer[d]) for d in (1, 3)]

    def pass_on(i, columns, copies):
        copies[0].wait_recv()
        a = same(row(i, 3, columns, 0), outer[1])
        copies[1].wait_recv()
        b = same(row(i, 1, columns, 1), outer[3])
        return [a, b]

    def to_twin(i, d):
        return same(row(i, d, whole), twin)

    def arrive(n, c):
        return pltpu.make_async_remote_copy(
            kv_send.at[0], kv_all.at[core, line, 0, n, c], kvs.at[0], kvr.at[n, c],
            device_id=twin, device_id_type=MESH,
        )

    rows_in, twin_in, own_in = [], [], []
    for i in range(4):
        for c in range(2):
            if i or c:
                arrive(i, c).wait_recv()
            else:
                pl.when(core == 1)(arrive(i, c).wait_recv)
        rows_in.append(
            [
                send(row(i, 0, own), row(i, 0, (4 - d, 1)), inner[d])
                for d in (2, 1, 3)
            ]
        )
        own_in.append(spread(i, own))
    q_copies = []
    for o in far_first:
        c = pltpu.make_async_remote_copy(
            q_send.at[lax.rem(z + o, 8)], q_all.at[8 - o],
            qs.at[o], qr.at[8 - o], device_id=along_z(o), device_id_type=MESH,
        )
        c.start()
        q_copies.append(c)
    ring_in, last = [], []

    def widen(i):
        for c in rows_in[i]:
            c.wait_recv()
        ring_in.append(spread(i, others))
        twin_in.append(to_twin(i, 0))
        last.append([])

    def turn(i):
        last[i] += pass_on(i, others, ring_in[i])
        twin_in.append(to_twin(i, 3))
        twin_in.append(to_twin(i, 1))

    def finish(i):
        for c in last[i]:
            c.wait_recv()
        twin_in.append(to_twin(i, 2))

    for i in range(4):
        widen(i)
    for i in range(4):
        last[i] += pass_on(i, own, own_in[i])
    for i in range(4):
        turn(i)
    for i in range(4):
        finish(i)
    for c in twin_in:
        c.wait_recv()
    for c in q_copies:
        c.wait_recv()

    def sort(i, carry):
        for u in range(16):
            p = i * 16 + u
            b = order[0, p]
            spot_of = (b >> 7, (b >> 5) & 3, (b >> 3) & 3, (b >> 1) & 3, b & 1)
            keys[p + REACH, :, pl.ds(0, DIM)] = kv_all[*spot_of, 0]
            vals[p + REACH, :, pl.ds(0, DIM)] = kv_all[*spot_of, 1]
        return carry

    lax.fori_loop(0, BLOCKS // 16, sort, 0)

    lane = lax.broadcasted_iota(jnp.int32, (N_ROWS, DIM), 1)
    causal = lane <= step // GROUP

    def window(ref, o, c0, width):
        blocks = ref[pl.ds(block_at(o) + c0 // TOK, width // TOK)]
        return blocks.reshape(width, 2 * DIM)

    def score(o, slot, first=0, n=N_ROWS):
        part = slice(first, first + n)
        q = jnp.concatenate([q_all[o, part], q_doc[o, part]], axis=1)
        top = jnp.full((n, DIM), LOW, jnp.float32)
        for c0 in range(0, PAD, CHUNK):
            width = min(CHUNK, PAD - c0)
            s = lax.dot_general(
                q, window(keys, o, c0, width), (((1,), (1,)), ((), ())),
                preferred_element_type=jnp.float32,
            )
            for t in range(0, width, DIM):
                tile = s[:, t : t + DIM]
                if c0 + t == REACH * TOK:
                    tile = jnp.where(causal[part], tile, LOW)
                scores[slot, :n, c0 + t : c0 + t + DIM] = tile
                top = jnp.maximum(top, tile)
        peaks[slot, :n] = jnp.broadcast_to(jnp.max(top, axis=1, keepdims=True), (n, DIM))

    def weigh(o, slot, peak, first=0, n=N_ROWS):
        total = jnp.zeros((n, 2 * DIM), jnp.float32)
        for c0 in range(0, PAD, CHUNK):
            width = min(CHUNK, PAD - c0)
            tiles = [
                jnp.exp2((scores[slot, :n, c0 + t : c0 + t + DIM] - peak) * FACTOR)
                for t in range(0, width, DIM)
            ]
            w = jnp.concatenate([tile.astype(jnp.bfloat16) for tile in tiles], axis=1)
            total = total + jnp.dot(
                w, window(vals, o, c0, width), preferred_element_type=jnp.float32
            )
        o_send[o, first : first + n] = (total[:, :DIM] / total[:, DIM:]).astype(jnp.bfloat16)

    def home_copy(o):
        return pltpu.make_async_remote_copy(
            o_send.at[o], o_all.at[z], os.at[o], orr.at[lax.rem(8 - o, 8)],
            device_id=along_z(o), device_id_type=MESH,
        )

    def half_copy(o, h):
        part = pl.ds(h * HALF, HALF)
        return pltpu.make_async_remote_copy(
            o_send.at[o, part], o_all.at[z, part], os.at[o + 8 * h], orr.at[8 - o + 8 * h],
            device_id=along_z(o), device_id_type=MESH,
        )

    split = (4, 3)
    halves = [(o, h) for o in split for h in range(2)]
    score(halves[0][0], 0, 0, HALF)
    for n, (o, h) in enumerate(halves):
        peak = peaks[n % 2, :HALF]
        if n + 1 < len(halves):
            score(halves[n + 1][0], 1 - n % 2, halves[n + 1][1] * HALF, HALF)
        else:
            score(5, 0)
        weigh(o, n % 2, peak, h * HALF, HALF)
        half_copy(o, h).start()

    def two(i, carry):
        peak = peaks[0]
        score(2 - i, 1)
        weigh(5 + i, 0, peak)
        home_copy(5 + i).start()
        peak = peaks[1]
        score(jnp.minimum(6 + i, 7), 0)
        weigh(2 - i, 1, peak)
        pl.when(i < 2)(home_copy(2 - i).start)
        return carry

    lax.fori_loop(0, 3, two, 0)
    o_all[z] = o_send[0]
    for o in far_first:
        if o in split:
            half_copy(o, 0).wait_recv()
            half_copy(o, 1).wait_recv()
        else:
            home_copy(o).wait_recv()
    for g in range(HEADS // 2):
        pair = [
            o_all[2 * g + i].astype(jnp.float32).reshape(TOK, GROUP, DIM) for i in range(2)
        ]
        out_ref[:, 16 * g : 16 * g + 16, :] = jnp.concatenate(pair, axis=1).astype(jnp.bfloat16)
    pl.when(core == 1)(beside.wait_send)
    for c in list(kv_copies.values()) + q_copies + sends:
        c.wait_send()
    for o in far_first:
        if o in split:
            half_copy(o, 0).wait_send()
            half_copy(o, 1).wait_send()
        else:
            home_copy(o).wait_send()


def shards(queries, keys, values, offsets, smooth_exp, scale_exp, placement, doc_lengths):
    bf, f32 = jnp.bfloat16, jnp.float32
    dma = pltpu.SemaphoreType.DMA
    hbm = pl.BlockSpec(memory_space=pltpu.HBM)
    return pl.pallas_call(
        kernel,
        out_shape=pltpu.VMEM(queries.shape, bf),
        in_specs=[hbm] * 8,
        out_specs=pl.BlockSpec(memory_space=pltpu.VMEM),
        scratch_shapes=[
            pltpu.VMEM((64, DIM), jnp.int32),
            pltpu.SMEM((64, DIM), jnp.int32),
            pltpu.SMEM((DOCS,), jnp.int32),
            pltpu.VMEM(queries.shape, bf),
            pltpu.VMEM(keys.shape, bf),
            pltpu.VMEM(values.shape, bf),
            pltpu.VMEM(offsets.shape, jnp.int32),
            pltpu.VMEM((HEADS, DIM), jnp.int32),
            pltpu.VMEM((HEADS, DIM), jnp.int32),
            pltpu.VMEM((1, BLOCKS), jnp.int32),
            pltpu.SMEM((1, BLOCKS), jnp.int32),
            pltpu.VMEM((2, TOK * HEADS, DIM), f32),
            pltpu.VMEM((HEADS, 2, TOK, DIM), bf),
            pltpu.VMEM((2, 4, 4, 4, 2, 2, TOK, DIM), bf),
            pltpu.VMEM((HEADS, N_ROWS, DIM), bf),
            pltpu.VMEM((8, N_ROWS, DIM), bf),
            pltpu.VMEM((8, N_ROWS, DIM), bf),
            pltpu.VMEM((8, N_ROWS, DIM), bf),
            pltpu.VMEM((HEADS, N_ROWS, DIM), bf),
            pltpu.VMEM((SORTED, TOK, 2 * DIM), bf),
            pltpu.VMEM((SORTED, TOK, 2 * DIM), bf),
            pltpu.VMEM((2, N_ROWS, PAD), f32),
            pltpu.VMEM((2, N_ROWS, DIM), f32),
            dma((8,)), dma((4, 2)), dma((8,)), dma((8,)), dma((16,)), dma((16,)),
            dma((60,)), dma((60,)), dma((10,)),
        ],
        compiler_params=pltpu.CompilerParams(
            collective_id=0, has_side_effects=True, vmem_limit_bytes=60 * 2**20
        ),
        name="attend",
    )(
        placement.reshape(64, DIM), doc_lengths, queries, keys, values, offsets, smooth_exp,
        scale_exp,
    )


def solution(mesh):
    tokens = P(("ctx", "kv"), None, None)
    return jax.shard_map(
        shards,
        mesh=mesh,
        in_specs=(tokens,) * 4 + (P(),) * 4,
        out_specs=tokens,
        check_vma=False,
    )
```
